256 devices in a mesh: row: 8 (over y, core), col: 8 (over z), depth: 4 (over x).
Axes of the slice: x: 4, y: 4, z: 8, core: 2. Of those that a mesh axis runs over, the one named last changes fastest.
Arguments:
- blocks: bfloat16 [512, 13, 128, 128], P(('row', 'col'), None, 'depth'), may hold values from -1.1953125 to 1.1953125
- pattern: int32 [512, 13], replicated, may hold values from 0 to 511, as said below
- place: int32 [512], replicated, may hold values from 0 to 511, as said below
Outputs:
- square: bfloat16 [512, 13, 128, 128], P(('row', 'col'), None, 'depth')
The draws below stay inside these ranges and needn't reach their ends.
Inputs may be any that keep to these rules, and one draw needn't show every extreme that they name: `place`: A permutation of the block rows; block j is stored in a slot s with (s // 8) mod 8 = j mod 8. `pattern`: row s lists the 13 distinct block columns of the block row b stored in slot s, in increasing order of their offset o in (b + o) mod 512, with offsets within -12 to 12, one of them 0; in every row at most 2 of the columns are equal mod 8, and some residue has exactly 2.
All inputs are finite; a program needn't handle non-finite values.
Results may differ from the reference program's by a relative error of at most 0.013.
Values may be sent and summed in bfloat16 or wider, within the bound.
A program may use at most 128 MiB of HBM per device.

```python
import jax
import jax.numpy as jnp
from jax import lax

BS = 128
ENTRIES = 13
REACH = 12
RD = 8
NB = 512
N_COL = 8
N_DEPTH = 4


def storage_layout(key):
    per_group = NB // N_COL
    group_keys = jax.random.split(key, N_COL)

    def shuffle(group_key):
        return jax.random.permutation(group_key, per_group)
    orders = jax.vmap(shuffle)(group_keys)
    block_ids = jnp.arange(NB, dtype=jnp.int32)
    col_group = block_ids % N_COL
    member = block_ids // N_COL
    position = orders[col_group, member].astype(jnp.int32)
    row_group = position // RD
    within = position % RD
    return ((row_group * N_COL + col_group) * RD + within).astype(jnp.int32)


def draw_place(key, part):
    return storage_layout(key)


def draw_pattern(key, part):
    layout = storage_layout(key)
    key = jax.random.fold_in(key, 7)
    window = 2 * REACH + 1
    capacity = (ENTRIES + N_COL - 1) // N_COL
    scores = jax.random.randint(key, (NB, window), 0, 2 ** 20) * 64 + jnp.arange(window, dtype=jnp.int32)[None, :]
    scores = scores.at[:, REACH].set(2 ** 28)
    offsets = jnp.arange(window, dtype=jnp.int32) - REACH
    block_base = jnp.arange(NB, dtype=jnp.int32)
    residue = (block_base[:, None] + offsets[None, :]) % N_COL
    same_class = residue[:, :, None] == residue[:, None, :]
    above = scores[:, None, :] > scores[:, :, None]
    rank_in = jnp.sum((same_class & above).astype(jnp.int32), axis=2)
    kept = jnp.where(rank_in < capacity, scores, -1)
    top_vals, top_index = lax.top_k(kept, ENTRIES)
    chosen = jnp.sort(top_index.astype(jnp.int32), axis=1) - REACH
    columns = ((block_base[:, None] + chosen) % NB).astype(jnp.int32)
    return jnp.zeros((NB, ENTRIES), jnp.int32).at[layout].set(columns)


def steps_of(key, extent, cuts, least, top_value):
    def one(dim, shards_of):
        steps = jax.random.uniform(jax.random.fold_in(jax.random.fold_in(key, 6), dim), (shards_of,), jnp.float32, least / len(cuts), top_value / len(cuts))
        return jnp.repeat(jnp.exp(steps), extent[dim] // shards_of).reshape((-1,) + (1,) * (len(extent) - dim - 1))

    level = one(*cuts[0])
    for cut in cuts[1:]:
        level = level * one(*cut)
    return level


def noise(stream_key, extent, deviation, most, pieces=(), held_as=jnp.bfloat16):
    array = jax.random.normal(stream_key, extent, jnp.float32) * deviation
    if len(pieces) > 0:
        array = steps_of(stream_key, extent, pieces, -0.22, 0.18) * array
    return jnp.clip(array, min=-most, max=most).astype(held_as)


def setup_inputs(seed: int = 0) -> dict:
    seeds = jax.random.split(jax.random.key(seed), 4)
    blocks = noise(seeds[0], (NB, ENTRIES, BS, BS), 0.2, 1.1953125, ((0, 64), (2, 4)))
    pattern = draw_pattern(jax.random.fold_in(seeds[3], 71), 0)
    place = draw_place(jax.random.fold_in(seeds[3], 71), 0)
    return dict(blocks=blocks, pattern=pattern, place=place)


def reference(blocks, pattern, place):
    quarter = BS // N_DEPTH

    def one_row(slot_id):
        own_blocks = blocks[slot_id].astype(jnp.float32)
        columns = pattern[slot_id]
        targets = place[columns]
        far_blocks = blocks[targets].astype(jnp.float32)
        far_cols = pattern[targets]
        matches = (columns[None, :, None] == far_cols[:, None, :]).astype(jnp.float32)
        aligned = jnp.einsum('axy,ayjs->axjs', matches, far_blocks)
        left_side = own_blocks.reshape(ENTRIES, N_DEPTH, quarter, BS)
        right_side = aligned.reshape(ENTRIES, ENTRIES, N_DEPTH, quarter, BS)
        partials = jnp.einsum('xdjr,axdjs->adrs', left_side, right_side)
        partials = partials.astype(jnp.bfloat16).astype(jnp.float32)
        return jnp.sum(partials, axis=1).astype(jnp.bfloat16)

    return lax.map(one_row, jnp.arange(NB, dtype=jnp.int32))
```

```python
import functools

import jax
import jax.numpy as jnp
from jax import lax
from jax.experimental import pallas as pl
from jax.experimental.pallas import tpu as pltpu
from jax.sharding import PartitionSpec as P

MESH = pl.DeviceIdType.MESH
F32 = jnp.float32
BF16 = jnp.bfloat16


def kernel(
    n_row, n_col, n_depth, rd, entries, cap,
    own_ref, meta_ref, out_ref,
    panel, lhs, part, half_in, full_in, back, pick_v, place_v, pick, place_s,
    y_send, y_recv, z_send, z_recv, h_send, h_recv, f_send, f_recv,
    b_send, b_recv, local_sem,
):
    r, c, d = lax.axis_index("row"), lax.axis_index("col"), lax.axis_index("depth")
    shard = rd * entries
    piece = shard // 2
    group = rd * n_col
    lanes = cap * group
    zero_block = n_row * shard
    blocks_unit = rd * cap

    def ring(me, step, size):
        return lax.rem(me + (step + size), size)

    def at_row(step):
        return (ring(r, step, n_row), c, d)

    def at_col(step):
        return (r, ring(c, step, n_col), d)

    def at_depth(step):
        return (r, c, ring(d, step, n_depth))

    far = n_col // 2
    barrier = pltpu.get_barrier_semaphore()
    partners = [at_row(1), at_row(-1), at_depth(1), at_depth(-1)]
    partners += [at_col(s) for s in range(1, n_col)]
    for other in partners:
        pl.semaphore_signal(barrier, inc=1, device_id=other, device_id_type=MESH)
    pl.semaphore_wait(barrier, len(partners))

    def y_copy(way, t, h):
        sign = 1 if way == 0 else -1
        owner = ring(r, -sign * (t - 1), n_row)
        span = pl.ds(owner * shard + h * piece, piece)
        src = own_ref.at[pl.ds(h * piece, piece)] if t == 1 else panel.at[span]
        return pltpu.make_async_remote_copy(
            src_ref=src, dst_ref=panel.at[span],
            send_sem=y_send.at[way, t - 1, h], recv_sem=y_recv.at[way, t - 1, h],
            device_id=at_row(sign), device_id_type=MESH,
        )

    def y_arrived(way, t, h):
        sign = 1 if way == 0 else -1
        owner = ring(r, -sign * t, n_row)
        span = pl.ds(owner * shard + h * piece, piece)
        pltpu.make_async_remote_copy(
            src_ref=panel.at[span], dst_ref=panel.at[span],
            send_sem=y_send.at[way, t - 1, h], recv_sem=y_recv.at[way, t - 1, h],
            device_id=at_row(sign), device_id_type=MESH,
        ).wait_recv()

    def z_unit(way, t):
        return 2 * t - 1 + (way if t < far else 0)

    def z_copy(way, t, h):
        sign = 1 if way == 0 else -1
        span = pl.ds(h * piece, piece)
        src = own_ref.at[span] if t == 1 else lhs.at[z_unit(way, t - 1) - 1, span]
        return pltpu.make_async_remote_copy(
            src_ref=src, dst_ref=lhs.at[z_unit(way, t) - 1, span],
            send_sem=z_send.at[way, t - 1, h], recv_sem=z_recv.at[way, t - 1, h],
            device_id=at_col(sign), device_id_type=MESH,
        )

    def used(t, way, h, size):
        return t < size // 2 or (t == size // 2 and h == way)

    def y_step(t, h):
        for way in range(2):
            if used(t, way, h, n_row):
                y_arrived(way, t, h)
                if used(t + 1, way, h, n_row):
                    y_copy(way, t + 1, h).start()

    def z_step(t, h):
        for way in range(2):
            if used(t, way, h, n_col):
                z_copy(way, t, h).wait_recv()
                if used(t + 1, way, h, n_col):
                    z_copy(way, t + 1, h).start()

    for h in range(2):
        for way in range(2):
            y_copy(way, 1, h).start()
            z_copy(way, 1, h).start()
    own_copy = pltpu.make_async_copy(
        own_ref, panel.at[pl.ds(r * shard, shard)], local_sem.at[0]
    )
    own_copy.start()
    panel[zero_block] = jnp.zeros((panel.shape[1], panel.shape[2]), BF16)

    nb = meta_ref.shape[0]
    lane_row = lax.broadcasted_iota(jnp.int32, (group, lanes), 1) % group
    pick_row = lax.broadcasted_iota(jnp.int32, (group, lanes), 0) == lane_row
    mine = meta_ref[pl.ds(pl.multiple_of(r * group, group), group), :]
    cols = [
        jnp.sum(jnp.where(pick_row, mine[:, x : x + 1], 0), axis=0, keepdims=True)
        for x in range(entries)
    ]
    lane = lax.broadcasted_iota(jnp.int32, (1, lanes), 1)
    rank = lane // group
    target = jnp.full((1, lanes), -1, jnp.int32)
    seen = jnp.zeros((1, lanes), jnp.int32)
    for x in range(entries):
        hit = lax.rem(cols[x], n_col) == c
        target = jnp.where(hit & (seen == rank), cols[x], target)
        seen = seen + hit.astype(jnp.int32)
    ids = lax.broadcasted_iota(jnp.int32, (nb, lanes), 0)
    slot = jnp.sum(
        jnp.where(ids == target, meta_ref[:, entries : entries + 1], 0), axis=0, keepdims=True
    )
    at_slot = ids == slot
    base = (slot // group * rd + lax.rem(slot, rd)) * entries
    found = [jnp.full((1, lanes), zero_block, jnp.int32) for _ in range(entries)]
    for y in range(entries):
        far_col = jnp.sum(
            jnp.where(at_slot, meta_ref[:, y : y + 1], 0), axis=0, keepdims=True
        )
        for x in range(entries):
            found[x] = jnp.where(
                (cols[x] == far_col) & (target >= 0), base + y, found[x]
            )
    for x in range(entries):
        pick_v[pl.ds(x, 1), :] = found[x]

    own_rows = meta_ref[pl.ds(pl.multiple_of((r * n_col + c) * rd, rd), rd), :]
    width = own_rows.shape[1]
    kind = lax.rem(own_rows, n_col)
    entry = lax.broadcasted_iota(jnp.int32, (rd, width), 1)
    before = jnp.zeros((rd, width), jnp.int32)
    for x in range(entries):
        before = before + ((kind == kind[:, x : x + 1]) & (entry > x)).astype(jnp.int32)
    home = kind * blocks_unit + lax.broadcasted_iota(jnp.int32, (rd, width), 0) * cap + before
    place_v[:, pl.ds(0, width)] = home
    pick_copy = pltpu.make_async_copy(pick_v, pick, local_sem.at[1])
    place_copy = pltpu.make_async_copy(place_v, place_s, local_sem.at[2])
    pick_copy.start()
    place_copy.start()

    def offset(u):
        if u == 0:
            return 0
        t = (u + 1) // 2
        return -t if u % 2 == 1 else t

    quarter = panel.shape[1]

    def multiply(u):
        source = ring(c, offset(u), n_col)

        def one_row(w, carry):
            n = source * rd + w
            if u == 0:
                left = own_ref[pl.ds(w * entries, entries)]
            else:
                left = lhs[u - 1, pl.ds(w * entries, entries)]
            left = left.reshape(entries * quarter, left.shape[2])
            right = jnp.concatenate(
                [
                    jnp.concatenate(
                        [panel[pick[x, m * group + n]] for x in range(entries)], axis=0
                    )
                    for m in range(cap)
                ],
                axis=1,
            )
            product = lax.dot_general(
                left, right, (((0,), (0,)), ((), ())), preferred_element_type=F32
            ).astype(BF16)
            width = left.shape[1]
            for q in range(n_depth):
                for m in range(cap):
                    part[u, q, w * cap + m] = product[
                        q * quarter : (q + 1) * quarter, m * width : (m + 1) * width
                    ]
            return carry

        lax.fori_loop(0, rd, one_row, 0)

    mid = blocks_unit // 2
    spans = (pl.ds(0, mid), pl.ds(mid, mid))

    def half_copy(u, way):
        return pltpu.make_async_remote_copy(
            src_ref=part.at[u, ring(d, 2, n_depth), spans[way]],
            dst_ref=half_in.at[u, way],
            send_sem=h_send.at[u, way], recv_sem=h_recv.at[u, way],
            device_id=at_depth(1 if way == 0 else -1), device_id_type=MESH,
        )

    def full_copy(u, way):
        step = 1 if way == 0 else -1
        return pltpu.make_async_remote_copy(
            src_ref=part.at[u, ring(d, step, n_depth)],
            dst_ref=full_in.at[u, way],
            send_sem=f_send.at[u, way], recv_sem=f_recv.at[u, way],
            device_id=at_depth(step), device_id_type=MESH,
        )

    def back_copy(u, home_of):
        span = pl.ds(home_of * blocks_unit, blocks_unit)
        return pltpu.make_async_remote_copy(
            src_ref=part.at[u, d], dst_ref=back.at[span],
            send_sem=b_send.at[u], recv_sem=b_recv.at[u],
            device_id=at_col(offset(u)), device_id_type=MESH,
        )

    def first(u):
        for way in range(2):
            half_copy(u, way).start()

    def second(u):
        for way in range(2):
            half_copy(u, way).wait_recv()
            q = ring(d, 1 if way == 0 else -1, n_depth)
            total = part[u, q, spans[way]].astype(F32) + half_in[u, way].astype(F32)
            part[u, q, spans[way]] = total.astype(BF16)
            full_copy(u, way).start()

    def third(u):
        for way in range(2):
            full_copy(u, way).wait_recv()
        total = part[u, d].astype(F32) + full_in[u, 0].astype(F32) + full_in[u, 1].astype(F32)
        if u == 0:
            back[pl.ds(c * blocks_unit, blocks_unit)] = total.astype(BF16)
        else:
            part[u, d] = total.astype(BF16)
            back_copy(u, c).start()

    y_step(1, 0)
    y_step(1, 1)
    z_step(1, 0)
    y_step(2, 0)
    y_step(2, 1)
    z_step(1, 1)
    y_step(3, 0)
    y_step(3, 1)
    z_step(2, 0)
    y_step(4, 0)
    y_step(4, 1)
    own_copy.wait()
    pick_copy.wait()
    place_copy.wait()

    multiply(0)
    first(0)
    multiply(1)
    first(1)
    second(0)
    z_step(2, 1)
    multiply(2)
    first(2)
    second(1)
    third(0)
    multiply(3)
    first(3)
    second(2)
    third(1)
    z_step(3, 0)
    multiply(4)
    first(4)
    second(3)
    third(2)
    z_step(3, 1)
    multiply(5)
    first(5)
    second(4)
    third(3)
    multiply(6)
    first(6)
    second(5)
    third(4)
    z_step(4, 0)
    z_step(4, 1)
    multiply(7)
    first(7)
    second(6)
    third(5)
    second(7)
    third(6)
    third(7)

    for u in range(1, n_col):
        back_copy(u, ring(c, -offset(u), n_col)).wait_recv()
    for w in range(rd):
        for a in range(entries):
            out_ref[w * entries + a] = back[place_s[w, a]]

    for way in range(2):
        for t in range(1, far + 1):
            for h in range(2):
                if used(t, way, h, n_row):
                    y_copy(way, t, h).wait_send()
                if used(t, way, h, n_col):
                    z_copy(way, t, h).wait_send()
        for u in range(n_col):
            half_copy(u, way).wait_send()
            full_copy(u, way).wait_send()
    for u in range(1, n_col):
        back_copy(u, c).wait_send()


def solution(mesh):
    n_row, n_col, n_depth = mesh.shape["row"], mesh.shape["col"], mesh.shape["depth"]

    def body(blocks, pattern, place):
        rd, entries, quarter, width = blocks.shape
        cap = (entries + n_col - 1) // n_col
        shard, unit = rd * entries, rd * cap
        lanes = cap * rd * n_col
        meta = jnp.concatenate([pattern, place[:, None]], axis=1)
        dma, vmem = pltpu.SemaphoreType.DMA, pltpu.VMEM
        result = pl.pallas_call(
            functools.partial(kernel, n_row, n_col, n_depth, rd, entries, cap),
            out_shape=jax.ShapeDtypeStruct((shard, quarter, width), BF16),
            in_specs=[pl.BlockSpec(memory_space=pltpu.VMEM)] * 2,
            out_specs=pl.BlockSpec(memory_space=pltpu.VMEM),
            scratch_shapes=[
                vmem((n_row * shard + 1, quarter, width), BF16),
                vmem((n_col - 1, shard, quarter, width), BF16),
                vmem((n_col, n_depth, unit, quarter, width), BF16),
                vmem((n_col, 2, unit // 2, quarter, width), BF16),
                vmem((n_col, 2, unit, quarter, width), BF16),
                vmem((n_col * unit, quarter, width), BF16),
                vmem((16, lanes), jnp.int32),
                vmem((8, 128), jnp.int32),
                pltpu.SMEM((16, lanes), jnp.int32),
                pltpu.SMEM((8, 128), jnp.int32),
                dma((2, n_row // 2, 2)), dma((2, n_row // 2, 2)),
                dma((2, n_col // 2, 2)), dma((2, n_col // 2, 2)),
                dma((n_col, 2)), dma((n_col, 2)),
                dma((n_col, 2)), dma((n_col, 2)),
                dma((n_col,)), dma((n_col,)),
                dma((3,)),
            ],
            compiler_params=pltpu.CompilerParams(
                collective_id=0, has_side_effects=True, vmem_limit_bytes=48 * 2**20
            ),
        )(blocks.reshape(shard, quarter, width), meta)
        return result.reshape(blocks.shape)

    placed = (P(("row", "col"), None, "depth", None), P(), P())
    return jax.shard_map(
        body,
        mesh=mesh,
        in_specs=placed,
        out_specs=P(("row", "col"), None, "depth", None),
        check_vma=False,
    )
```

```python
import functools

import jax
import jax.numpy as jnp
from jax import lax
from jax.experimental import pallas as pl
from jax.experimental.pallas import tpu as pltpu
from jax.sharding import PartitionSpec as P

MESH = pl.DeviceIdType.MESH
F32 = jnp.float32
BF16 = jnp.bfloat16
REACH = 3
PIECES = 4


def kernel(
    n_row, n_col, n_depth, rd, entries, cap,
    own_ref, pattern_ref, place_ref, out_ref,
    panel, panel2, lhs, part, half_in, full_in, back,
    pattern_v, place_v, meta, pick_v, home_v, pick, home,
    y_send, y_recv, y4_send, y4_recv, z_send, z_recv,
    v_send, v_recv, v4_send, v4_recv,
    h_send, h_recv, f_send, f_recv, b_send, b_recv, local_sem,
):
    r, c, d = lax.axis_index("row"), lax.axis_index("col"), lax.axis_index("depth")
    core, odd = lax.rem(r, 2), lax.rem(c, 2)
    shard = rd * entries
    piece = shard // PIECES
    half = shard // 2
    group = rd * n_col
    lanes = cap * group
    zero_block = n_row * shard
    unit = rd * cap
    far = n_col // 2

    def ring(me, step, size):
        return lax.rem(me + step + size, size)

    def at_row(step):
        return (ring(r, step, n_row), c, d)

    def at_col(step):
        return (r, ring(c, step, n_col), d)

    def at_depth(step):
        return (r, c, ring(d, step, n_depth))

    def remote(src, dst, send, recv, to):
        return pltpu.make_async_remote_copy(
            src_ref=src, dst_ref=dst, send_sem=send, recv_sem=recv,
            device_id=to, device_id_type=MESH,
        )

    partners = [at_row(1), at_row(-1), at_depth(1), at_depth(-1)]
    partners += [at_col(s) for s in range(-REACH, REACH + 1) if s != 0]
    pattern_copy = pltpu.make_async_copy(pattern_ref, pattern_v, local_sem.at[3])
    place_copy = pltpu.make_async_copy(place_ref, place_v, local_sem.at[4])
    own_copy = pltpu.make_async_copy(
        own_ref, panel.at[pl.ds(r * shard, shard)], local_sem.at[0]
    )
    pattern_copy.start()
    place_copy.start()
    own_copy.start()
    barrier = pltpu.get_barrier_semaphore()
    for other in partners:
        pl.semaphore_signal(barrier, inc=1, device_id=other, device_id_type=MESH)
    pl.semaphore_wait(barrier, len(partners))

    signs = (1, -1)
    side = 1 - 2 * core

    def span_of(owner, p, size):
        return pl.ds(owner * shard + p * size, size)

    def y_copy(way, t, h, owner_step):
        span = span_of(ring(r, owner_step, n_row), h, half)
        src = own_ref.at[pl.ds(h * half, half)] if t == 1 else panel.at[span]
        return remote(
            src, panel.at[span], y_send.at[way, t - 1, h], y_recv.at[way, t - 1, h],
            at_row(signs[way]),
        )

    def y_out(way, t, h):
        return y_copy(way, t, h, -signs[way] * (t - 1))

    def y_in(way, t, h):
        span = span_of(ring(r, -signs[way] * t, n_row), h, half)
        remote(
            panel.at[span], panel.at[span], y_send.at[way, t - 1, h],
            y_recv.at[way, t - 1, h], at_row(signs[way]),
        ).wait_recv()

    def y4_copy(h, owner):
        span = span_of(owner, h, half)
        return remote(
            panel.at[span], panel.at[span], y4_send.at[h], y4_recv.at[h], at_row(side)
        )

    def y4_out(h):
        return y4_copy(h, ring(r, -3 * side, n_row))

    def y_step(t, h):
        for way in range(2):
            y_in(way, t, h)
            if t < 3:
                y_out(way, t + 1, h).start()
        if t == 3:
            y4_out(h).start()

    mate = 1 - odd

    def v_out(way, t, p):
        span = span_of(ring(r, -signs[way] * (t - 1), n_row), p, piece)
        src = lhs.at[mate, pl.ds(p * piece, piece)] if t == 1 else panel2.at[span]
        return remote(
            src, panel2.at[span], v_send.at[way, t - 1, p], v_recv.at[way, t - 1, p],
            at_row(signs[way]),
        )

    def v_in(way, t, p):
        span = span_of(ring(r, -signs[way] * t, n_row), p, piece)
        remote(
            panel2.at[span], panel2.at[span], v_send.at[way, t - 1, p],
            v_recv.at[way, t - 1, p], at_row(signs[way]),
        ).wait_recv()

    def v4_copy(p, owner):
        span = span_of(owner, p, piece)
        return remote(
            panel2.at[span], panel2.at[span], v4_send.at[p], v4_recv.at[p], at_row(side)
        )

    def v4_out(p):
        return v4_copy(p, ring(r, -3 * side, n_row))

    def v_first(p):
        for way in range(2):
            v_out(way, 1, p).start()

    def v_step(t, p):
        for way in range(2):
            v_in(way, t, p)
            if t < 3:
                v_out(way, t + 1, p).start()
        if t == 3:
            v4_out(p).start()

    def z_copy(way, t, p):
        span = pl.ds(p * piece, piece)
        src = own_ref.at[span] if t == 1 else lhs.at[2 * t - 4 + way, span]
        return remote(
            src, lhs.at[2 * t - 2 + way, span],
            z_send.at[way, t - 1, p], z_recv.at[way, t - 1, p], at_col(signs[way]),
        )

    def z_first(p):
        for way in range(2):
            z_copy(way, 1, p).start()

    def z_step(t, p):
        for way in range(2):
            z_copy(way, t, p).wait_recv()
            if t < REACH:
                z_copy(way, t + 1, p).start()

    for h in range(2):
        for way in range(2):
            y_out(way, 1, h).start()
        z_first(h)
    panel[zero_block] = jnp.zeros((panel.shape[1], panel.shape[2]), BF16)
    panel2[zero_block] = jnp.zeros((panel.shape[1], panel.shape[2]), BF16)

    nb = meta.shape[0]
    pattern_copy.wait()
    place_copy.wait()
    pad = jnp.zeros((128 - entries - 1, nb), jnp.int32)
    meta[...] = jnp.transpose(
        jnp.concatenate([pattern_v[...], place_v[...], pad], axis=0)
    )[:, : meta.shape[1]]
    partner = c + 1 - 2 * odd
    opposite = ring(c, far, n_col)
    visitor = ring(partner, far, n_col)
    lane_of = lax.broadcasted_iota(jnp.int32, (group, lanes), 1) % group
    lane_row = jnp.where(lane_of // rd == opposite, lane_of + (visitor - opposite) * rd, lane_of)
    pick_row = lax.broadcasted_iota(jnp.int32, (group, lanes), 0) == lane_row
    mine = meta[pl.ds(pl.multiple_of(r * group, group), group), :]
    cols = [
        jnp.sum(jnp.where(pick_row, mine[:, x : x + 1], 0), axis=0, keepdims=True)
        for x in range(entries)
    ]
    lane = lax.broadcasted_iota(jnp.int32, (1, lanes), 1)
    rank = lane // group
    wanted = jnp.where((lane % group) // rd == opposite, partner, c)
    target = jnp.full((1, lanes), -1, jnp.int32)
    seen = jnp.zeros((1, lanes), jnp.int32)
    for x in range(entries):
        hit = lax.rem(cols[x], n_col) == wanted
        target = jnp.where(hit & (seen == rank), cols[x], target)
        seen = seen + hit.astype(jnp.int32)
    ids = lax.broadcasted_iota(jnp.int32, (nb, lanes), 0)
    slot = jnp.sum(
        jnp.where(ids == target, meta[:, entries : entries + 1], 0), axis=0, keepdims=True
    )
    at_slot = ids == slot
    base = (slot // group * rd + lax.rem(slot, rd)) * entries
    found = [jnp.full((1, lanes), zero_block, jnp.int32) for _ in range(entries)]
    for y in range(entries):
        far_col = jnp.sum(
            jnp.where(at_slot, meta[:, y : y + 1], 0), axis=0, keepdims=True
        )
        for x in range(entries):
            found[x] = jnp.where(
                (cols[x] == far_col) & (target >= 0), base + y, found[x]
            )
    for x in range(entries):
        pick_v[pl.ds(x, 1), :] = found[x]

    own_rows = meta[pl.ds(pl.multiple_of((r * n_col + c) * rd, rd), rd), :]
    width = own_rows.shape[1]
    kind = lax.rem(own_rows, n_col)
    entry = lax.broadcasted_iota(jnp.int32, (rd, width), 1)
    before = jnp.zeros((rd, width), jnp.int32)
    for x in range(entries):
        before = before + ((kind == kind[:, x : x + 1]) & (entry > x)).astype(jnp.int32)
    spot = kind * unit + lax.broadcasted_iota(jnp.int32, (rd, width), 0) * cap + before
    home_v[:, pl.ds(0, width)] = spot
    pick_copy = pltpu.make_async_copy(pick_v, pick, local_sem.at[1])
    home_copy = pltpu.make_async_copy(home_v, home, local_sem.at[2])
    pick_copy.start()
    home_copy.start()

    def offset(u):
        t = (u + 1) // 2
        return 0 if u == 0 else (far if t == far else (-t if u % 2 == 1 else t))

    quarter = panel.shape[1]
    rows_h = rd // 2
    blocks_h = unit // 2

    def multiply(u, h):
        source = ring(c, offset(u), n_col)
        table = panel if u < n_col - 1 else panel2

        def one_row(w, carry):
            n = source * rd + w
            if u == 0:
                left = panel[pl.ds(r * shard + w * entries, entries)]
            elif u < n_col - 1:
                left = lhs[u - 1, pl.ds(w * entries, entries)]
            else:
                left = lhs[2 * REACH - 2 + odd, pl.ds(w * entries, entries)]
            left = left.reshape(entries * quarter, left.shape[2])
            right = jnp.concatenate(
                [
                    jnp.concatenate(
                        [table[pick[x, m * group + n]] for x in range(entries)], axis=0
                    )
                    for m in range(cap)
                ],
                axis=1,
            )
            product = lax.dot_general(
                left, right, (((0,), (0,)), ((), ())), preferred_element_type=F32
            ).astype(BF16)
            width = left.shape[1]
            for q in range(n_depth):
                for m in range(cap):
                    part[u, q, w * cap + m] = product[
                        q * quarter : (q + 1) * quarter, m * width : (m + 1) * width
                    ]
            return carry

        lax.fori_loop(h * rows_h, (h + 1) * rows_h, one_row, 0)

    mid = blocks_h // 2

    def mids(h, way):
        return pl.ds(h * blocks_h + way * mid, mid)

    def half_copy(u, h, way):
        return remote(
            part.at[u, ring(d, 2, n_depth), mids(h, way)], half_in.at[u, mids(h, way)],
            h_send.at[u, h, way], h_recv.at[u, h, way], at_depth(signs[way]),
        )

    def full_copy(u, h, way):
        span = pl.ds(h * blocks_h, blocks_h)
        return remote(
            part.at[u, ring(d, signs[way], n_depth), span], full_in.at[u, way, span],
            f_send.at[u, h, way], f_recv.at[u, h, way], at_depth(signs[way]),
        )

    def shift(u):
        return 2 * REACH * odd - REACH if u == n_col - 1 else offset(u)

    def back_copy(u, h, kind_of):
        span = pl.ds(kind_of * unit + h * blocks_h, blocks_h)
        return remote(
            part.at[u, d, pl.ds(h * blocks_h, blocks_h)], back.at[span],
            b_send.at[u, h], b_recv.at[u, h], at_col(shift(u)),
        )

    def back_out(u, h):
        return back_copy(u, h, partner if u == n_col - 1 else c)

    def first(u, h):
        for way in range(2):
            half_copy(u, h, way).start()

    def second(u, h):
        for way in range(2):
            half_copy(u, h, way).wait_recv()
            q = ring(d, signs[way], n_depth)
            total = part[u, q, mids(h, way)].astype(F32) + half_in[u, mids(h, way)].astype(F32)
            part[u, q, mids(h, way)] = total.astype(BF16)
            full_copy(u, h, way).start()

    def third(u, h):
        for way in range(2):
            full_copy(u, h, way).wait_recv()
        span = pl.ds(h * blocks_h, blocks_h)
        total = (
            part[u, d, span].astype(F32)
            + full_in[u, 0, span].astype(F32)
            + full_in[u, 1, span].astype(F32)
        ).astype(BF16)
        if u == 0:
            back[pl.ds(c * unit + h * blocks_h, blocks_h)] = total
        else:
            part[u, d, span] = total

    items = [(0, 0), (0, 1)] + [(u, 0) for u in range(1, 7)]
    items += [(u, 1) for u in range(1, 7)] + [(7, 0), (7, 1)]
    done = {"mul": 0, "second": 0, "third": 0, "back": 0}

    def work(n=1):
        for _ in range(n):
            k = done["mul"]
            if k < len(items):
                multiply(*items[k])
                first(*items[k])
                done["mul"] = k + 1

    def add(n=1):
        for _ in range(n):
            k = done["second"]
            if k < done["mul"]:
                second(*items[k])
                done["second"] = k + 1

    def finish(n=1):
        for _ in range(n):
            k = done["third"]
            if k < done["second"]:
                third(*items[k])
                done["third"] = k + 1

    def give():
        while done["back"] < done["third"]:
            item = items[done["back"]]
            if item[0] > 0:
                back_out(*item).start()
            done["back"] += 1

    y_step(1, 0)
    z_step(1, 0)
    y_step(1, 1)
    z_step(1, 1)
    y_step(2, 0)
    z_step(2, 0)
    y_step(2, 1)
    z_step(2, 1)
    y_step(3, 0)
    z_step(3, 0)
    z_first(2)
    z_first(3)
    v_first(0)
    v_first(1)
    y_step(3, 1)
    z_step(3, 1)
    own_copy.wait()
    pick_copy.wait()
    home_copy.wait()
    for h in range(2):
        y4_copy(h, ring(r, 4, n_row)).wait_recv()

    work()
    v_step(1, 0)
    work(2)
    add()
    z_step(1, 2)
    v_step(1, 1)
    work()
    add()
    work()
    v_step(2, 0)
    finish()
    add()
    work()
    add()
    z_step(1, 3)
    pltpu.make_async_copy(
        lhs.at[mate], panel2.at[pl.ds(r * shard, shard)], local_sem.at[5]
    ).start()
    v_step(2, 1)
    finish()
    work()
    add()
    work()
    finish()
    v_step(3, 0)
    v_first(2)
    v_first(3)
    work()
    add()
    finish()
    z_step(2, 2)
    v_step(3, 1)
    work()
    add()
    finish()
    v_step(1, 2)
    add()
    finish()
    z_step(2, 3)
    v_step(1, 3)
    work()
    add()
    finish()
    work()
    v_step(2, 2)
    add()
    finish()
    z_step(3, 2)
    v_step(2, 3)
    add()
    finish()
    v_step(3, 2)
    add()
    finish()
    z_step(3, 3)
    finish()
    give()
    work()
    add()
    finish()
    work()
    v_step(3, 3)
    pltpu.make_async_copy(
        lhs.at[mate], panel2.at[pl.ds(r * shard, shard)], local_sem.at[5]
    ).wait()
    for p in range(PIECES):
        v4_copy(p, ring(r, 4, n_row)).wait_recv()
    work()
    add()
    finish()
    give()
    work()
    for _ in range(len(items)):
        add()
        finish()
        give()

    for u in range(1, n_col):
        for h in range(2):
            kind_of = ring(c, -offset(u), n_col)
            back_copy(u, h, kind_of).wait_recv()
    for w in range(rd):
        for a in range(entries):
            out_ref[w * entries + a] = back[home[w, a]]

    for way in range(2):
        for t in range(1, REACH + 1):
            for h in range(2):
                y_out(way, t, h).wait_send()
            for p in range(PIECES):
                z_copy(way, t, p).wait_send()
                v_out(way, t, p).wait_send()
        for u in range(n_col):
            for h in range(2):
                half_copy(u, h, way).wait_send()
                full_copy(u, h, way).wait_send()
    for h in range(2):
        y4_out(h).wait_send()
        for u in range(1, n_col):
            back_out(u, h).wait_send()
    for p in range(PIECES):
        v4_out(p).wait_send()


def solution(mesh):
    n_row, n_col, n_depth = mesh.shape["row"], mesh.shape["col"], mesh.shape["depth"]

    def body(blocks, pattern, place):
        rd, entries, quarter, width = blocks.shape
        nb = pattern.shape[0]
        cap = (entries + n_col - 1) // n_col
        shard, unit = rd * entries, rd * cap
        lanes = cap * rd * n_col
        dma, vmem, ints = pltpu.SemaphoreType.DMA, pltpu.VMEM, jnp.int32
        result = pl.pallas_call(
            functools.partial(kernel, n_row, n_col, n_depth, rd, entries, cap),
            out_shape=jax.ShapeDtypeStruct((shard, quarter, width), BF16),
            in_specs=[pl.BlockSpec(memory_space=pl.ANY)] * 3,
            out_specs=pl.BlockSpec(memory_space=pltpu.VMEM),
            scratch_shapes=[
                vmem((n_row * shard + 1, quarter, width), BF16),
                vmem((n_row * shard + 1, quarter, width), BF16),
                vmem((2 * REACH, shard, quarter, width), BF16),
                vmem((n_col, n_depth, unit, quarter, width), BF16),
                vmem((n_col, unit, quarter, width), BF16),
                vmem((n_col, 2, unit, quarter, width), BF16),
                vmem((n_col * unit, quarter, width), BF16),
                vmem((entries, nb), ints), vmem((1, nb), ints), vmem((nb, 16), ints),
                vmem((16, lanes), ints), vmem((8, 128), ints),
                pltpu.SMEM((16, lanes), ints), pltpu.SMEM((8, 128), ints),
                dma((2, 3, 2)), dma((2, 3, 2)), dma((2,)), dma((2,)),
                dma((2, REACH, PIECES)), dma((2, REACH, PIECES)),
                dma((2, 3, PIECES)), dma((2, 3, PIECES)), dma((PIECES,)), dma((PIECES,)),
                dma((n_col, 2, 2)), dma((n_col, 2, 2)),
                dma((n_col, 2, 2)), dma((n_col, 2, 2)),
                dma((n_col, 2)), dma((n_col, 2)),
                dma((6,)),
            ],
            compiler_params=pltpu.CompilerParams(
                collective_id=0, has_side_effects=True, vmem_limit_bytes=62 * 2**20
            ),
        )(blocks.reshape(shard, quarter, width), pattern.T, place.reshape(1, nb))
        return result.reshape(blocks.shape)

    placed = (P(("row", "col"), None, "depth", None), P(), P())
    return jax.shard_map(
        body,
        mesh=mesh,
        in_specs=placed,
        out_specs=P(("row", "col"), None, "depth", None),
        check_vma=False,
    )
```

```python
import functools

import jax
import jax.numpy as jnp
from jax import lax
from jax.experimental import pallas as pl
from jax.experimental.pallas import tpu as pltpu
from jax.sharding import PartitionSpec as P

MESH = pl.DeviceIdType.MESH
F32 = jnp.float32
BF16 = jnp.bfloat16
REACH = 3
PIECES = 4

ORDER = (
    ("idx",), ("y", 1, 0), ("z", 1, 0), ("y", 1, 1), ("z", 1, 1), ("y", 2, 0), ("z", 2, 0),
    ("zf", 2), ("y", 2, 1), ("z", 2, 1), ("zf", 3), ("y", 3, 0), ("z", 3, 0), ("vf", 0),
    ("vf", 1), ("y", 3, 1), ("z", 1, 2), ("panel",), ("mul", 3, 0), ("v", 1, 0), ("mul", 4, 0),
    ("v", 1, 1), ("z", 3, 1), ("mul", 5, 0), ("add", 3, 0), ("mul", 6, 0), ("add", 4, 0),
    ("v", 2, 0), ("mul", 1, 0), ("z", 1, 3), ("v", 2, 1), ("add", 5, 0), ("add", 6, 0),
    ("end", 3, 0), ("mul", 2, 0), ("v", 3, 0), ("vf", 2), ("vf", 3), ("z", 2, 2),
    ("add", 1, 0), ("end", 5, 0), ("end", 4, 0), ("v", 3, 1), ("mul", 1, 1), ("add", 2, 0),
    ("end", 6, 0), ("mul", 2, 1), ("z", 2, 3), ("v", 1, 2), ("give", 5, 0), ("add", 1, 1),
    ("v", 1, 3), ("give", 6, 0), ("give", 3, 0), ("give", 4, 0), ("end", 1, 0), ("give", 1, 0),
    ("end", 2, 0), ("add", 2, 1), ("give", 2, 0), ("mul", 3, 1), ("z", 3, 2), ("mul", 4, 1),
    ("v", 2, 2), ("end", 1, 1), ("give", 1, 1), ("mul", 0, 0), ("v", 2, 3), ("add", 3, 1),
    ("z", 3, 3), ("add", 4, 1), ("end", 2, 1), ("give", 2, 1), ("mul", 5, 1), ("v", 3, 2),
    ("add", 0, 0), ("mul", 6, 1), ("v", 3, 3), ("end", 3, 1), ("give", 3, 1), ("end", 4, 1),
    ("give", 4, 1), ("add", 5, 1), ("panel2",), ("mul", 7, 0), ("mul", 7, 1), ("add", 6, 1),
    ("end", 0, 0), ("end", 5, 1), ("give", 5, 1), ("mul", 0, 1), ("add", 7, 0), ("add", 7, 1),
    ("end", 6, 1), ("give", 6, 1), ("add", 0, 1), ("end", 7, 0), ("give", 7, 0), ("end", 7, 1),
    ("give", 7, 1), ("end", 0, 1),
)


def kernel(
    n_row, n_col, n_depth, rd, entries, cap,
    own_ref, pattern_ref, place_ref, out_ref,
    panel, panel2, lhs, part, half_in, full_in, back,
    pattern_v, place_v, meta, pick_v, home_v, pick, home,
    y_send, y_recv, y4_send, y4_recv, z_send, z_recv,
    v_send, v_recv, v4_send, v4_recv,
    h_send, h_recv, f_send, f_recv, b_send, b_recv, local_sem,
):
    r, c, d = lax.axis_index("row"), lax.axis_index("col"), lax.axis_index("depth")
    core, odd = lax.rem(r, 2), lax.rem(c, 2)
    shard = rd * entries
    piece = shard // PIECES
    half = shard // 2
    group = rd * n_col
    lanes = cap * group
    zero_block = n_row * shard
    unit = rd * cap
    far = n_col // 2

    def ring(me, step, size):
        return lax.rem(me + step + size, size)

    def at_row(step):
        return (ring(r, step, n_row), c, d)

    def at_col(step):
        return (r, ring(c, step, n_col), d)

    def at_depth(step):
        return (r, c, ring(d, step, n_depth))

    def remote(src, dst, send, recv, to):
        return pltpu.make_async_remote_copy(
            src_ref=src, dst_ref=dst, send_sem=send, recv_sem=recv,
            device_id=to, device_id_type=MESH,
        )

    partners = [at_row(1), at_row(-1), at_depth(1), at_depth(-1)]
    partners += [at_col(s) for s in range(-REACH, REACH + 1) if s != 0]
    pattern_copy = pltpu.make_async_copy(pattern_ref, pattern_v, local_sem.at[3])
    place_copy = pltpu.make_async_copy(place_ref, place_v, local_sem.at[4])
    own_copy = pltpu.make_async_copy(
        own_ref, panel.at[pl.ds(r * shard, shard)], local_sem.at[0]
    )
    pattern_copy.start()
    place_copy.start()
    own_copy.start()
    barrier = pltpu.get_barrier_semaphore()
    for other in partners:
        pl.semaphore_signal(barrier, inc=1, device_id=other, device_id_type=MESH)
    pl.semaphore_wait(barrier, len(partners))

    signs = (1, -1)
    side = 1 - 2 * core

    def span_of(owner, p, size):
        return pl.ds(owner * shard + p * size, size)

    def y_copy(way, t, h, owner_step):
        span = span_of(ring(r, owner_step, n_row), h, half)
        src = own_ref.at[pl.ds(h * half, half)] if t == 1 else panel.at[span]
        return remote(
            src, panel.at[span], y_send.at[way, t - 1, h], y_recv.at[way, t - 1, h],
            at_row(signs[way]),
        )

    def y_out(way, t, h):
        return y_copy(way, t, h, -signs[way] * (t - 1))

    def y_in(way, t, h):
        span = span_of(ring(r, -signs[way] * t, n_row), h, half)
        remote(
            panel.at[span], panel.at[span], y_send.at[way, t - 1, h],
            y_recv.at[way, t - 1, h], at_row(signs[way]),
        ).wait_recv()

    def y4_copy(h, owner):
        span = span_of(owner, h, half)
        return remote(
            panel.at[span], panel.at[span], y4_send.at[h], y4_recv.at[h], at_row(side)
        )

    def y4_out(h):
        return y4_copy(h, ring(r, -3 * side, n_row))

    def y_step(t, h):
        for way in range(2):
            y_in(way, t, h)
            if t < 3:
                y_out(way, t + 1, h).start()
        if t == 3:
            y4_out(h).start()

    mate = 1 - odd

    def v_out(way, t, p):
        span = span_of(ring(r, -signs[way] * (t - 1), n_row), p, piece)
        src = lhs.at[mate, pl.ds(p * piece, piece)] if t == 1 else panel2.at[span]
        return remote(
            src, panel2.at[span], v_send.at[way, t - 1, p], v_recv.at[way, t - 1, p],
            at_row(signs[way]),
        )

    def v_in(way, t, p):
        span = span_of(ring(r, -signs[way] * t, n_row), p, piece)
        remote(
            panel2.at[span], panel2.at[span], v_send.at[way, t - 1, p],
            v_recv.at[way, t - 1, p], at_row(signs[way]),
        ).wait_recv()

    def v4_copy(p, owner):
        span = span_of(owner, p, piece)
        return remote(
            panel2.at[span], panel2.at[span], v4_send.at[p], v4_recv.at[p], at_row(side)
        )

    def v4_out(p):
        return v4_copy(p, ring(r, -3 * side, n_row))

    def v_first(p):
        for way in range(2):
            v_out(way, 1, p).start()

    def v_step(t, p):
        for way in range(2):
            v_in(way, t, p)
            if t < 3:
                v_out(way, t + 1, p).start()
        if t == 3:
            v4_out(p).start()

    def z_copy(way, t, p):
        span = pl.ds(p * piece, piece)
        src = own_ref.at[span] if t == 1 else lhs.at[2 * t - 4 + way, span]
        return remote(
            src, lhs.at[2 * t - 2 + way, span],
            z_send.at[way, t - 1, p], z_recv.at[way, t - 1, p], at_col(signs[way]),
        )

    def z_first(p):
        for way in range(2):
            z_copy(way, 1, p).start()

    def z_step(t, p):
        for way in range(2):
            z_copy(way, t, p).wait_recv()
            if t < REACH:
                z_copy(way, t + 1, p).start()

    for h in range(2):
        for way in range(2):
            y_out(way, 1, h).start()
        z_first(h)
    panel[zero_block] = jnp.zeros((panel.shape[1], panel.shape[2]), BF16)
    panel2[zero_block] = jnp.zeros((panel.shape[1], panel.shape[2]), BF16)

    nb = meta.shape[0]
    pattern_copy.wait()
    place_copy.wait()
    pad = jnp.zeros((128 - entries - 1, nb), jnp.int32)
    meta[...] = jnp.transpose(
        jnp.concatenate([pattern_v[...], place_v[...], pad], axis=0)
    )[:, : meta.shape[1]]
    partner = c + 1 - 2 * odd
    opposite = ring(c, far, n_col)
    visitor = ring(partner, far, n_col)
    lane_of = lax.broadcasted_iota(jnp.int32, (group, lanes), 1) % group
    lane_row = jnp.where(lane_of // rd == opposite, lane_of + (visitor - opposite) * rd, lane_of)
    pick_row = lax.broadcasted_iota(jnp.int32, (group, lanes), 0) == lane_row
    mine = meta[pl.ds(pl.multiple_of(r * group, group), group), :]
    cols = [
        jnp.sum(jnp.where(pick_row, mine[:, x : x + 1], 0), axis=0, keepdims=True)
        for x in range(entries)
    ]
    lane = lax.broadcasted_iota(jnp.int32, (1, lanes), 1)
    rank = lane // group
    wanted = jnp.where((lane % group) // rd == opposite, partner, c)
    target = jnp.full((1, lanes), -1, jnp.int32)
    seen = jnp.zeros((1, lanes), jnp.int32)
    for x in range(entries):
        hit = lax.rem(cols[x], n_col) == wanted
        target = jnp.where(hit & (seen == rank), cols[x], target)
        seen = seen + hit.astype(jnp.int32)
    ids = lax.broadcasted_iota(jnp.int32, (nb, lanes), 0)
    slot = jnp.sum(
        jnp.where(ids == target, meta[:, entries : entries + 1], 0), axis=0, keepdims=True
    )
    at_slot = ids == slot
    base = (slot // group * rd + lax.rem(slot, rd)) * entries
    found = [jnp.full((1, lanes), zero_block, jnp.int32) for _ in range(entries)]
    for y in range(entries):
        far_col = jnp.sum(
            jnp.where(at_slot, meta[:, y : y + 1], 0), axis=0, keepdims=True
        )
        for x in range(entries):
            found[x] = jnp.where(
                (cols[x] == far_col) & (target >= 0), base + y, found[x]
            )
    for x in range(entries):
        pick_v[pl.ds(x, 1), :] = found[x]

    own_rows = meta[pl.ds(pl.multiple_of((r * n_col + c) * rd, rd), rd), :]
    width = own_rows.shape[1]
    kind = lax.rem(own_rows, n_col)
    entry = lax.broadcasted_iota(jnp.int32, (rd, width), 1)
    before = jnp.zeros((rd, width), jnp.int32)
    for x in range(entries):
        before = before + ((kind == kind[:, x : x + 1]) & (entry > x)).astype(jnp.int32)
    spot = kind * unit + lax.broadcasted_iota(jnp.int32, (rd, width), 0) * cap + before
    home_v[:, pl.ds(0, width)] = spot
    pick_copy = pltpu.make_async_copy(pick_v, pick, local_sem.at[1])
    home_copy = pltpu.make_async_copy(home_v, home, local_sem.at[2])
    pick_copy.start()
    home_copy.start()

    def offset(u):
        t = (u + 1) // 2
        return 0 if u == 0 else (far if t == far else (-t if u % 2 == 1 else t))

    quarter = panel.shape[1]
    rows_h = rd // 2
    blocks_h = unit // 2

    def multiply(u, h):
        source = ring(c, offset(u), n_col)
        table = panel if u < n_col - 1 else panel2

        def one_row(w, carry):
            n = source * rd + w
            if u == 0:
                left = panel[pl.ds(r * shard + w * entries, entries)]
            elif u < n_col - 1:
                left = lhs[u - 1, pl.ds(w * entries, entries)]
            else:
                left = lhs[2 * REACH - 2 + odd, pl.ds(w * entries, entries)]
            left = left.reshape(entries * quarter, left.shape[2])
            right = jnp.concatenate(
                [
                    jnp.concatenate(
                        [table[pick[x, m * group + n]] for x in range(entries)], axis=0
                    )
                    for m in range(cap)
                ],
                axis=1,
            )
            product = lax.dot_general(
                left, right, (((0,), (0,)), ((), ())), preferred_element_type=F32
            ).astype(BF16)
            width = left.shape[1]
            for q in range(n_depth):
                for m in range(cap):
                    part[u, q, w * cap + m] = product[
                        q * quarter : (q + 1) * quarter, m * width : (m + 1) * width
                    ]
            return carry

        lax.fori_loop(h * rows_h, (h + 1) * rows_h, one_row, 0)

    mid = blocks_h // 2

    def mids(h, way):
        return pl.ds(h * blocks_h + way * mid, mid)

    def half_copy(u, h, way):
        return remote(
            part.at[u, ring(d, 2, n_depth), mids(h, way)], half_in.at[u, mids(h, way)],
            h_send.at[u, h, way], h_recv.at[u, h, way], at_depth(signs[way]),
        )

    def full_copy(u, h, way):
        span = pl.ds(h * blocks_h, blocks_h)
        return remote(
            part.at[u, ring(d, signs[way], n_depth), span], full_in.at[u, way, span],
            f_send.at[u, h, way], f_recv.at[u, h, way], at_depth(signs[way]),
        )

    def shift(u):
        return 2 * REACH * odd - REACH if u == n_col - 1 else offset(u)

    def back_copy(u, h, kind_of):
        span = pl.ds(kind_of * unit + h * blocks_h, blocks_h)
        return remote(
            part.at[u, d, pl.ds(h * blocks_h, blocks_h)], back.at[span],
            b_send.at[u, h], b_recv.at[u, h], at_col(shift(u)),
        )

    def back_out(u, h):
        return back_copy(u, h, partner if u == n_col - 1 else c)

    def first(u, h):
        for way in range(2):
            half_copy(u, h, way).start()

    def second(u, h):
        for way in range(2):
            half_copy(u, h, way).wait_recv()
            q = ring(d, signs[way], n_depth)
            total = part[u, q, mids(h, way)].astype(F32) + half_in[u, mids(h, way)].astype(F32)
            part[u, q, mids(h, way)] = total.astype(BF16)
            full_copy(u, h, way).start()

    def third(u, h):
        for way in range(2):
            full_copy(u, h, way).wait_recv()
        span = pl.ds(h * blocks_h, blocks_h)
        total = (
            part[u, d, span].astype(F32)
            + full_in[u, 0, span].astype(F32)
            + full_in[u, 1, span].astype(F32)
        ).astype(BF16)
        if u == 0:
            back[pl.ds(c * unit + h * blocks_h, blocks_h)] = total
        else:
            part[u, d, span] = total

    mate_copy = pltpu.make_async_copy(
        lhs.at[mate], panel2.at[pl.ds(r * shard, shard)], local_sem.at[5]
    )
    here = []

    def z_event(t, p):
        z_step(t, p)
        if t == 1:
            here.append(p)
            if len(here) == PIECES:
                mate_copy.start()

    def whole_panel():
        own_copy.wait()
        pick_copy.wait()
        home_copy.wait()
        for h in range(2):
            y4_copy(h, ring(r, 4, n_row)).wait_recv()

    def whole_panel2():
        mate_copy.wait()
        for p in range(PIECES):
            v4_copy(p, ring(r, 4, n_row)).wait_recv()

    def mul(u, h):
        multiply(u, h)
        first(u, h)

    steps = {
        "y": y_step, "z": z_event, "zf": z_first, "v": v_step, "vf": v_first,
        "panel": whole_panel, "panel2": whole_panel2,
        "mul": mul, "add": second, "end": third,
        "give": lambda u, h: back_out(u, h).start(),
    }
    for step in ORDER:
        if step[0] != "idx":
            steps[step[0]](*step[1:])

    for u in range(1, n_col):
        for h in range(2):
            kind_of = ring(c, -offset(u), n_col)
            back_copy(u, h, kind_of).wait_recv()
    for w in range(rd):
        for a in range(entries):
            out_ref[w * entries + a] = back[home[w, a]]

    for way in range(2):
        for t in range(1, REACH + 1):
            for h in range(2):
                y_out(way, t, h).wait_send()
            for p in range(PIECES):
                z_copy(way, t, p).wait_send()
                v_out(way, t, p).wait_send()
        for u in range(n_col):
            for h in range(2):
                half_copy(u, h, way).wait_send()
                full_copy(u, h, way).wait_send()
    for h in range(2):
        y4_out(h).wait_send()
        for u in range(1, n_col):
            back_out(u, h).wait_send()
    for p in range(PIECES):
        v4_out(p).wait_send()


def solution(mesh):
    n_row, n_col, n_depth = mesh.shape["row"], mesh.shape["col"], mesh.shape["depth"]

    def body(blocks, pattern, place):
        rd, entries, quarter, width = blocks.shape
        nb = pattern.shape[0]
        cap = (entries + n_col - 1) // n_col
        shard, unit = rd * entries, rd * cap
        lanes = cap * rd * n_col
        dma, vmem, ints = pltpu.SemaphoreType.DMA, pltpu.VMEM, jnp.int32
        result = pl.pallas_call(
            functools.partial(kernel, n_row, n_col, n_depth, rd, entries, cap),
            out_shape=jax.ShapeDtypeStruct((shard, quarter, width), BF16),
            in_specs=[pl.BlockSpec(memory_space=pltpu.HBM)] * 3,
            out_specs=pl.BlockSpec(memory_space=pltpu.VMEM),
            scratch_shapes=[
                vmem((n_row * shard + 1, quarter, width), BF16),
                vmem((n_row * shard + 1, quarter, width), BF16),
                vmem((2 * REACH, shard, quarter, width), BF16),
                vmem((n_col, n_depth, unit, quarter, width), BF16),
                vmem((n_col, unit, quarter, width), BF16),
                vmem((n_col, 2, unit, quarter, width), BF16),
                vmem((n_col * unit, quarter, width), BF16),
                vmem((entries, nb), ints), vmem((1, nb), ints), vmem((nb, 16), ints),
                vmem((16, lanes), ints), vmem((8, 128), ints),
                pltpu.SMEM((16, lanes), ints), pltpu.SMEM((8, 128), ints),
                dma((2, 3, 2)), dma((2, 3, 2)), dma((2,)), dma((2,)),
                dma((2, REACH, PIECES)), dma((2, REACH, PIECES)),
                dma((2, 3, PIECES)), dma((2, 3, PIECES)), dma((PIECES,)), dma((PIECES,)),
                dma((n_col, 2, 2)), dma((n_col, 2, 2)),
                dma((n_col, 2, 2)), dma((n_col, 2, 2)),
                dma((n_col, 2)), dma((n_col, 2)),
                dma((6,)),
            ],
            compiler_params=pltpu.CompilerParams(
                collective_id=0, has_side_effects=True, vmem_limit_bytes=62 * 2**20
            ),
        )(blocks.reshape(shard, quarter, width), pattern.T, place.reshape(1, nb))
        return result.reshape(blocks.shape)

    placed = (P(("row", "col"), None, "depth", None), P(), P())
    return jax.shard_map(
        body,
        mesh=mesh,
        in_specs=placed,
        out_specs=P(("row", "col"), None, "depth", None),
        check_vma=False,
    )
```

```python
import functools

import jax
import jax.numpy as jnp
from jax import lax
from jax.experimental import pallas as pl
from jax.experimental.pallas import tpu as pltpu
from jax.sharding import PartitionSpec as P

MESH = pl.DeviceIdType.MESH
F32 = jnp.float32
BF16 = jnp.bfloat16
REACH = 3
PIECES = 4

ORDER = (
    ("index", 0), ("index", 1), ("index", 2), ("index", 3), ("y", 1, 0), ("z", 1, 0),
    ("y", 1, 1), ("z", 1, 1), ("y", 2, 0), ("z", 2, 0), ("zf", 2), ("y", 2, 1), ("z", 2, 1),
    ("zf", 3), ("y", 3, 0), ("z", 3, 0), ("vf", 0), ("vf", 1), ("y", 3, 1), ("z", 1, 2),
    ("panel",), ("mul", 3, 0), ("v", 1, 0), ("mul", 4, 0), ("v", 1, 1), ("z", 3, 1),
    ("mul", 5, 0), ("add", 3, 0), ("mul", 6, 0), ("add", 4, 0), ("v", 2, 0), ("mul", 1, 0),
    ("z", 1, 3), ("v", 2, 1), ("add", 5, 0), ("add", 6, 0), ("end", 3, 0), ("mul", 2, 0),
    ("v", 3, 0), ("vf", 2), ("vf", 3), ("z", 2, 2), ("add", 1, 0), ("end", 5, 0),
    ("end", 4, 0), ("v", 3, 1), ("mul", 1, 1), ("add", 2, 0), ("end", 6, 0), ("mul", 2, 1),
    ("z", 2, 3), ("v", 1, 2), ("give", 5, 0), ("add", 1, 1), ("v", 1, 3), ("give", 6, 0),
    ("give", 3, 0), ("give", 4, 0), ("end", 1, 0), ("give", 1, 0), ("end", 2, 0),
    ("add", 2, 1), ("give", 2, 0), ("mul", 3, 1), ("z", 3, 2), ("mul", 4, 1), ("v", 2, 2),
    ("end", 1, 1), ("give", 1, 1), ("mul", 0, 0), ("v", 2, 3), ("add", 3, 1), ("z", 3, 3),
    ("add", 4, 1), ("end", 2, 1), ("give", 2, 1), ("mul", 5, 1), ("v", 3, 2), ("add", 0, 0),
    ("mul", 6, 1), ("v", 3, 3), ("end", 3, 1), ("give", 3, 1), ("end", 4, 1), ("give", 4, 1),
    ("add", 5, 1), ("panel2",), ("mul", 7, 0), ("mul", 7, 1), ("add", 6, 1), ("end", 0, 0),
    ("end", 5, 1), ("give", 5, 1), ("mul", 0, 1), ("add", 7, 0), ("add", 7, 1), ("end", 6, 1),
    ("give", 6, 1), ("add", 0, 1), ("end", 7, 0), ("give", 7, 0), ("end", 7, 1),
    ("give", 7, 1), ("end", 0, 1),
)


def kernel(
    n_row, n_col, n_depth, rd, entries, cap,
    own_ref, pattern_ref, place_ref, out_ref,
    panel, panel2, lhs, part, half_in, full_in, back,
    pattern_v, place_v, meta, pick_v, home_v, pick, home,
    y_send, y_recv, y4_send, y4_recv, z_send, z_recv,
    v_send, v_recv, v4_send, v4_recv,
    h_send, h_recv, f_send, f_recv, b_send, b_recv, local_sem,
):
    r, c, d = lax.axis_index("row"), lax.axis_index("col"), lax.axis_index("depth")
    core, odd = lax.rem(r, 2), lax.rem(c, 2)
    shard = rd * entries
    piece = shard // PIECES
    half = shard // 2
    group = rd * n_col
    lanes = cap * group
    zero_block = n_row * shard
    unit = rd * cap
    far = n_col // 2

    def ring(me, step, size):
        return lax.rem(me + step + size, size)

    def at_row(step):
        return (ring(r, step, n_row), c, d)

    def at_col(step):
        return (r, ring(c, step, n_col), d)

    def at_depth(step):
        return (r, c, ring(d, step, n_depth))

    def remote(src, dst, send, recv, to):
        return pltpu.make_async_remote_copy(
            src_ref=src, dst_ref=dst, send_sem=send, recv_sem=recv,
            device_id=to, device_id_type=MESH,
        )

    partners = [at_row(1), at_row(-1), at_depth(1), at_depth(-1)]
    partners += [at_col(1), at_col(-1)]
    pattern_copy = pltpu.make_async_copy(pattern_ref, pattern_v, local_sem.at[3])
    place_copy = pltpu.make_async_copy(place_ref, place_v, local_sem.at[4])
    own_copy = pltpu.make_async_copy(
        own_ref, panel.at[pl.ds(r * shard, shard)], local_sem.at[0]
    )
    pattern_copy.start()
    place_copy.start()
    own_copy.start()
    barrier = pltpu.get_barrier_semaphore()
    for other in partners:
        pl.semaphore_signal(barrier, inc=1, device_id=other, device_id_type=MESH)
    pl.semaphore_wait(barrier, len(partners))

    signs = (1, -1)
    side = 1 - 2 * core

    def span_of(owner, p, size):
        return pl.ds(owner * shard + p * size, size)

    def y_copy(way, t, h, owner_step):
        span = span_of(ring(r, owner_step, n_row), h, half)
        src = own_ref.at[pl.ds(h * half, half)] if t == 1 else panel.at[span]
        return remote(
            src, panel.at[span], y_send.at[way, t - 1, h], y_recv.at[way, t - 1, h],
            at_row(signs[way]),
        )

    def y_out(way, t, h):
        return y_copy(way, t, h, -signs[way] * (t - 1))

    def y_in(way, t, h):
        span = span_of(ring(r, -signs[way] * t, n_row), h, half)
        remote(
            panel.at[span], panel.at[span], y_send.at[way, t - 1, h],
            y_recv.at[way, t - 1, h], at_row(signs[way]),
        ).wait_recv()

    def y4_copy(h, owner):
        span = span_of(owner, h, half)
        return remote(
            panel.at[span], panel.at[span], y4_send.at[h], y4_recv.at[h], at_row(side)
        )

    def y4_out(h):
        return y4_copy(h, ring(r, -3 * side, n_row))

    def y_step(t, h):
        for way in range(2):
            y_in(way, t, h)
            if t < 3:
                y_out(way, t + 1, h).start()
        if t == 3:
            y4_out(h).start()

    mate = 1 - odd

    def v_out(way, t, p):
        span = span_of(ring(r, -signs[way] * (t - 1), n_row), p, piece)
        src = lhs.at[mate, pl.ds(p * piece, piece)] if t == 1 else panel2.at[span]
        return remote(
            src, panel2.at[span], v_send.at[way, t - 1, p], v_recv.at[way, t - 1, p],
            at_row(signs[way]),
        )

    def v_in(way, t, p):
        span = span_of(ring(r, -signs[way] * t, n_row), p, piece)
        remote(
            panel2.at[span], panel2.at[span], v_send.at[way, t - 1, p],
            v_recv.at[way, t - 1, p], at_row(signs[way]),
        ).wait_recv()

    def v4_copy(p, owner):
        span = span_of(owner, p, piece)
        return remote(
            panel2.at[span], panel2.at[span], v4_send.at[p], v4_recv.at[p], at_row(side)
        )

    def v4_out(p):
        return v4_copy(p, ring(r, -3 * side, n_row))

    def v_first(p):
        for way in range(2):
            v_out(way, 1, p).start()

    def v_step(t, p):
        for way in range(2):
            v_in(way, t, p)
            if t < 3:
                v_out(way, t + 1, p).start()
        if t == 3:
            v4_out(p).start()

    def z_copy(way, t, p):
        span = pl.ds(p * piece, piece)
        src = own_ref.at[span] if t == 1 else lhs.at[2 * t - 4 + way, span]
        return remote(
            src, lhs.at[2 * t - 2 + way, span],
            z_send.at[way, t - 1, p], z_recv.at[way, t - 1, p], at_col(signs[way]),
        )

    def z_first(p):
        for way in range(2):
            z_copy(way, 1, p).start()

    def z_step(t, p):
        for way in range(2):
            z_copy(way, t, p).wait_recv()
            if t < REACH:
                z_copy(way, t + 1, p).start()

    for h in range(2):
        for way in range(2):
            y_out(way, 1, h).start()
        z_first(h)
    panel[zero_block] = jnp.zeros((panel.shape[1], panel.shape[2]), BF16)
    panel2[zero_block] = jnp.zeros((panel.shape[1], panel.shape[2]), BF16)

    nb = meta.shape[0]
    partner = c + 1 - 2 * odd
    opposite = ring(c, far, n_col)
    visitor = ring(partner, far, n_col)
    pick_copy = pltpu.make_async_copy(pick_v, pick, local_sem.at[1])
    home_copy = pltpu.make_async_copy(home_v, home, local_sem.at[2])
    table = {}

    def index_targets():
        pattern_copy.wait()
        place_copy.wait()
        pad = jnp.zeros((128 - entries - 1, nb), jnp.int32)
        meta[...] = jnp.transpose(
            jnp.concatenate([pattern_v[...], place_v[...], pad], axis=0)
        )[:, : meta.shape[1]]
        lane_of = lax.broadcasted_iota(jnp.int32, (group, lanes), 1) % group
        lane_row = jnp.where(
            lane_of // rd == opposite, lane_of + (visitor - opposite) * rd, lane_of
        )
        pick_row = lax.broadcasted_iota(jnp.int32, (group, lanes), 0) == lane_row
        mine = meta[pl.ds(pl.multiple_of(r * group, group), group), :]
        cols = [
            jnp.sum(jnp.where(pick_row, mine[:, x : x + 1], 0), axis=0, keepdims=True)
            for x in range(entries)
        ]
        lane = lax.broadcasted_iota(jnp.int32, (1, lanes), 1)
        rank = lane // group
        wanted = jnp.where((lane % group) // rd == opposite, partner, c)
        target = jnp.full((1, lanes), -1, jnp.int32)
        seen = jnp.zeros((1, lanes), jnp.int32)
        for x in range(entries):
            hit = lax.rem(cols[x], n_col) == wanted
            target = jnp.where(hit & (seen == rank), cols[x], target)
            seen = seen + hit.astype(jnp.int32)
        ids = lax.broadcasted_iota(jnp.int32, (nb, lanes), 0)
        table["slot"] = jnp.sum(
            jnp.where(ids == target, meta[:, entries : entries + 1], 0), axis=0, keepdims=True
        )
        table["cols"], table["target"] = cols, target
        table["found"] = [jnp.full((1, lanes), zero_block, jnp.int32) for _ in cols]

    def index_matches(low, high):
        slot, cols, target = table["slot"], table["cols"], table["target"]
        at_slot = lax.broadcasted_iota(jnp.int32, (nb, lanes), 0) == slot
        base = (slot // group * rd + lax.rem(slot, rd)) * entries
        for y in range(low, high):
            far_col = jnp.sum(
                jnp.where(at_slot, meta[:, y : y + 1], 0), axis=0, keepdims=True
            )
            table["found"] = [
                jnp.where((cols[x] == far_col) & (target >= 0), base + y, table["found"][x])
                for x in range(entries)
            ]

    def index_home():
        for x in range(entries):
            pick_v[pl.ds(x, 1), :] = table["found"][x]
        own_rows = meta[pl.ds(pl.multiple_of((r * n_col + c) * rd, rd), rd), :]
        width = own_rows.shape[1]
        kind = lax.rem(own_rows, n_col)
        entry = lax.broadcasted_iota(jnp.int32, (rd, width), 1)
        before = jnp.zeros((rd, width), jnp.int32)
        for x in range(entries):
            before = before + ((kind == kind[:, x : x + 1]) & (entry > x)).astype(jnp.int32)
        row = lax.broadcasted_iota(jnp.int32, (rd, width), 0)
        home_v[:, pl.ds(0, width)] = kind * unit + row * cap + before
        pick_copy.start()
        home_copy.start()

    index_steps = (
        index_targets,
        lambda: index_matches(0, entries // 2),
        lambda: index_matches(entries // 2, entries),
        index_home,
    )

    def offset(u):
        t = (u + 1) // 2
        return 0 if u == 0 else (far if t == far else (-t if u % 2 == 1 else t))

    quarter = panel.shape[1]
    rows_h = rd // 2
    blocks_h = unit // 2

    def multiply(u, h):
        source = ring(c, offset(u), n_col)
        source_panel = panel if u < n_col - 1 else panel2

        def one_row(w, carry):
            n = source * rd + w
            if u == 0:
                left = panel[pl.ds(r * shard + w * entries, entries)]
            elif u < n_col - 1:
                left = lhs[u - 1, pl.ds(w * entries, entries)]
            else:
                left = lhs[2 * REACH - 2 + odd, pl.ds(w * entries, entries)]
            left = left.reshape(entries * quarter, left.shape[2])
            right = jnp.concatenate(
                [
                    jnp.concatenate(
                        [source_panel[pick[x, m * group + n]] for x in range(entries)], axis=0
                    )
                    for m in range(cap)
                ],
                axis=1,
            )
            product = lax.dot_general(
                left, right, (((0,), (0,)), ((), ())), preferred_element_type=F32
            ).astype(BF16)
            width = left.shape[1]
            for q in range(n_depth):
                for m in range(cap):
                    part[u, q, w * cap + m] = product[
                        q * quarter : (q + 1) * quarter, m * width : (m + 1) * width
                    ]
            return carry

        lax.fori_loop(h * rows_h, (h + 1) * rows_h, one_row, 0)

    mid = blocks_h // 2

    def mids(h, way):
        return pl.ds(h * blocks_h + way * mid, mid)

    def half_copy(u, h, way):
        return remote(
            part.at[u, ring(d, 2, n_depth), mids(h, way)], half_in.at[u, mids(h, way)],
            h_send.at[u, h, way], h_recv.at[u, h, way], at_depth(signs[way]),
        )

    def full_copy(u, h, way):
        span = pl.ds(h * blocks_h, blocks_h)
        return remote(
            part.at[u, ring(d, signs[way], n_depth), span], full_in.at[u, way, span],
            f_send.at[u, h, way], f_recv.at[u, h, way], at_depth(signs[way]),
        )

    def shift(u):
        return 2 * REACH * odd - REACH if u == n_col - 1 else offset(u)

    def back_copy(u, h, kind_of):
        span = pl.ds(kind_of * unit + h * blocks_h, blocks_h)
        return remote(
            part.at[u, d, pl.ds(h * blocks_h, blocks_h)], back.at[span],
            b_send.at[u, h], b_recv.at[u, h], at_col(shift(u)),
        )

    def back_out(u, h):
        return back_copy(u, h, partner if u == n_col - 1 else c)

    def first(u, h):
        for way in range(2):
            half_copy(u, h, way).start()

    def second(u, h):
        for way in range(2):
            half_copy(u, h, way).wait_recv()
            q = ring(d, signs[way], n_depth)
            total = part[u, q, mids(h, way)].astype(F32) + half_in[u, mids(h, way)].astype(F32)
            part[u, q, mids(h, way)] = total.astype(BF16)
            full_copy(u, h, way).start()

    def third(u, h):
        for way in range(2):
            full_copy(u, h, way).wait_recv()
        span = pl.ds(h * blocks_h, blocks_h)
        total = (
            part[u, d, span].astype(F32)
            + full_in[u, 0, span].astype(F32)
            + full_in[u, 1, span].astype(F32)
        ).astype(BF16)
        if u == 0:
            back[pl.ds(c * unit + h * blocks_h, blocks_h)] = total
        else:
            part[u, d, span] = total

    mate_copy = pltpu.make_async_copy(
        lhs.at[mate], panel2.at[pl.ds(r * shard, shard)], local_sem.at[5]
    )
    here = []

    def z_event(t, p):
        z_step(t, p)
        if t == 1:
            here.append(p)
            if len(here) == PIECES:
                mate_copy.start()

    def whole_panel():
        own_copy.wait()
        pick_copy.wait()
        home_copy.wait()
        for h in range(2):
            y4_copy(h, ring(r, 4, n_row)).wait_recv()

    def whole_panel2():
        mate_copy.wait()
        for p in range(PIECES):
            v4_copy(p, ring(r, 4, n_row)).wait_recv()

    def mul(u, h):
        multiply(u, h)
        first(u, h)

    steps = {
        "y": y_step, "z": z_event, "zf": z_first, "v": v_step, "vf": v_first,
        "index": lambda k: index_steps[k](), "panel": whole_panel, "panel2": whole_panel2,
        "mul": mul, "add": second, "end": third,
        "give": lambda u, h: back_out(u, h).start(),
    }
    for step in ORDER:
        steps[step[0]](*step[1:])

    for way in range(2):
        for t in range(1, REACH + 1):
            for h in range(2):
                y_out(way, t, h).wait_send()
            for p in range(PIECES):
                z_copy(way, t, p).wait_send()
                v_out(way, t, p).wait_send()
        for u in range(n_col):
            for h in range(2):
                half_copy(u, h, way).wait_send()
                full_copy(u, h, way).wait_send()
    for h in range(2):
        y4_out(h).wait_send()
        for u in range(1, n_col):
            back_out(u, h).wait_send()
    for p in range(PIECES):
        v4_out(p).wait_send()

    for u in range(1, n_col):
        for h in range(2):
            kind_of = ring(c, -offset(u), n_col)
            back_copy(u, h, kind_of).wait_recv()
    for w in range(rd):
        for a in range(entries):
            out_ref[w * entries + a] = back[home[w, a]]


def solution(mesh):
    n_row, n_col, n_depth = mesh.shape["row"], mesh.shape["col"], mesh.shape["depth"]

    def body(blocks, pattern, place):
        rd, entries, quarter, width = blocks.shape
        nb = pattern.shape[0]
        cap = (entries + n_col - 1) // n_col
        shard, unit = rd * entries, rd * cap
        lanes = cap * rd * n_col
        dma, vmem, ints = pltpu.SemaphoreType.DMA, pltpu.VMEM, jnp.int32
        result = pl.pallas_call(
            functools.partial(kernel, n_row, n_col, n_depth, rd, entries, cap),
            out_shape=jax.ShapeDtypeStruct((shard, quarter, width), BF16),
            in_specs=[pl.BlockSpec(memory_space=pltpu.HBM)] * 3,
            out_specs=pl.BlockSpec(memory_space=pltpu.VMEM),
            scratch_shapes=[
                vmem((n_row * shard + 1, quarter, width), BF16),
                vmem((n_row * shard + 1, quarter, width), BF16),
                vmem((2 * REACH, shard, quarter, width), BF16),
                vmem((n_col, n_depth, unit, quarter, width), BF16),
                vmem((n_col, unit, quarter, width), BF16),
                vmem((n_col, 2, unit, quarter, width), BF16),
                vmem((n_col * unit, quarter, width), BF16),
                vmem((entries, nb), ints), vmem((1, nb), ints), vmem((nb, 16), ints),
                vmem((16, lanes), ints), vmem((8, 128), ints),
                pltpu.SMEM((16, lanes), ints), pltpu.SMEM((8, 128), ints),
                dma((2, 3, 2)), dma((2, 3, 2)), dma((2,)), dma((2,)),
                dma((2, REACH, PIECES)), dma((2, REACH, PIECES)),
                dma((2, 3, PIECES)), dma((2, 3, PIECES)), dma((PIECES,)), dma((PIECES,)),
                dma((n_col, 2, 2)), dma((n_col, 2, 2)),
                dma((n_col, 2, 2)), dma((n_col, 2, 2)),
                dma((n_col, 2)), dma((n_col, 2)),
                dma((6,)),
            ],
            compiler_params=pltpu.CompilerParams(
                collective_id=0, has_side_effects=True, vmem_limit_bytes=62 * 2**20
            ),
        )(blocks.reshape(shard, quarter, width), pattern.T, place.reshape(1, nb))
        return result.reshape(blocks.shape)

    placed = (P(("row", "col"), None, "depth", None), P(), P())
    return jax.shard_map(
        body,
        mesh=mesh,
        in_specs=placed,
        out_specs=P(("row", "col"), None, "depth", None),
        check_vma=False,
    )
```

```python
import functools

import jax
import jax.numpy as jnp
from jax import lax
from jax.experimental import pallas as pl
from jax.experimental.pallas import tpu as pltpu
from jax.sharding import PartitionSpec as P

MESH = pl.DeviceIdType.MESH
F32 = jnp.float32
BF16 = jnp.bfloat16
REACH = 3
PIECES = 4

ORDER = (
    ("index", 0), ("index", 1), ("index", 2), ("index", 3), ("y", 1, 0), ("z", 1, 0),
    ("y", 1, 1), ("z", 1, 1), ("y", 2, 0), ("z", 2, 0), ("zf", 2), ("y", 2, 1), ("z", 2, 1),
    ("zf", 3), ("y", 3, 0), ("z", 3, 0), ("vf", 0), ("vf", 1), ("y", 3, 1), ("z", 1, 2),
    ("panel",), ("mul", 1, 0), ("v", 1, 0), ("mul", 2, 0), ("mul", 3, 0), ("mul", 4, 0),
    ("mul", 0, 0), ("mul", 0, 1), ("z", 3, 1), ("v", 1, 1), ("add", 1, 0), ("mul", 5, 0),
    ("add", 2, 0), ("add", 3, 0), ("v", 2, 0), ("add", 4, 0), ("add", 0, 0), ("add", 0, 1),
    ("z", 1, 3), ("v", 2, 1), ("end", 1, 0), ("mul", 6, 0), ("add", 5, 0), ("mul", 1, 1),
    ("mul", 2, 1), ("v", 3, 0), ("vf", 2), ("vf", 3), ("end", 2, 0), ("end", 3, 0),
    ("z", 2, 2), ("v", 3, 1), ("end", 4, 0), ("end", 0, 0), ("v", 1, 2), ("end", 0, 1),
    ("z", 2, 3), ("add", 6, 0), ("give", 1, 0), ("give", 2, 0), ("give", 3, 0), ("give", 4, 0),
    ("mul", 3, 1), ("v", 1, 3), ("end", 5, 0), ("add", 1, 1), ("add", 2, 1), ("give", 5, 0),
    ("mul", 4, 1), ("v", 2, 2), ("end", 6, 0), ("z", 3, 2), ("give", 6, 0), ("add", 3, 1),
    ("v", 2, 3), ("end", 1, 1), ("give", 1, 1), ("end", 2, 1), ("give", 2, 1), ("add", 4, 1),
    ("v", 3, 2), ("z", 3, 3), ("mul", 5, 1), ("mul", 6, 1), ("end", 3, 1), ("give", 3, 1),
    ("v", 3, 3), ("end", 4, 1), ("give", 4, 1), ("panel2",), ("mul", 7, 0), ("mul", 7, 1),
    ("add", 5, 1), ("add", 6, 1), ("add", 7, 0), ("add", 7, 1), ("end", 5, 1), ("give", 5, 1),
    ("end", 6, 1), ("give", 6, 1), ("end", 7, 0), ("give", 7, 0), ("end", 7, 1),
    ("give", 7, 1),
)


def kernel(
    n_row, n_col, n_depth, rd, entries, cap,
    own_ref, pattern_ref, place_ref, out_ref,
    panel, panel2, lhs, part, half_in, full_in, back,
    pattern_v, place_v, meta, pick_v, home_v, pick, home,
    y_send, y_recv, y4_send, y4_recv, z_send, z_recv,
    v_send, v_recv, v4_send, v4_recv,
    h_send, h_recv, f_send, f_recv, b_send, b_recv, local_sem,
):
    r, c, d = lax.axis_index("row"), lax.axis_index("col"), lax.axis_index("depth")
    core, odd = lax.rem(r, 2), lax.rem(c, 2)
    shard = rd * entries
    piece = shard // PIECES
    half = shard // 2
    group = rd * n_col
    lanes = cap * group
    zero_block = n_row * shard
    unit = rd * cap
    far = n_col // 2

    def ring(me, step, size):
        return lax.rem(me + step + size, size)

    def at_row(step):
        return (ring(r, step, n_row), c, d)

    def at_col(step):
        return (r, ring(c, step, n_col), d)

    def at_depth(step):
        return (r, c, ring(d, step, n_depth))

    def remote(src, dst, send, recv, to):
        return pltpu.make_async_remote_copy(
            src_ref=src, dst_ref=dst, send_sem=send, recv_sem=recv,
            device_id=to, device_id_type=MESH,
        )

    partners = [at_row(1), at_row(-1), at_depth(1), at_depth(-1)]
    partners += [at_col(1), at_col(-1)]
    pattern_copy = pltpu.make_async_copy(pattern_ref, pattern_v, local_sem.at[3])
    place_copy = pltpu.make_async_copy(place_ref, place_v, local_sem.at[4])
    own_copy = pltpu.make_async_copy(
        own_ref, panel.at[pl.ds(r * shard, shard)], local_sem.at[0]
    )
    pattern_copy.start()
    place_copy.start()
    own_copy.start()
    barrier = pltpu.get_barrier_semaphore()
    for other in partners:
        pl.semaphore_signal(barrier, inc=1, device_id=other, device_id_type=MESH)
    pl.semaphore_wait(barrier, len(partners))

    signs = (1, -1)
    side = 1 - 2 * core

    def span_of(owner, p, size):
        return pl.ds(owner * shard + p * size, size)

    def y_copy(way, t, h, owner_step):
        span = span_of(ring(r, owner_step, n_row), h, half)
        src = own_ref.at[pl.ds(h * half, half)] if t == 1 else panel.at[span]
        return remote(
            src, panel.at[span], y_send.at[way, t - 1, h], y_recv.at[way, t - 1, h],
            at_row(signs[way]),
        )

    def y_out(way, t, h):
        return y_copy(way, t, h, -signs[way] * (t - 1))

    def y_in(way, t, h):
        span = span_of(ring(r, -signs[way] * t, n_row), h, half)
        remote(
            panel.at[span], panel.at[span], y_send.at[way, t - 1, h],
            y_recv.at[way, t - 1, h], at_row(signs[way]),
        ).wait_recv()

    def y4_copy(h, owner):
        span = span_of(owner, h, half)
        return remote(
            panel.at[span], panel.at[span], y4_send.at[h], y4_recv.at[h], at_row(side)
        )

    def y4_out(h):
        return y4_copy(h, ring(r, -3 * side, n_row))

    def y_step(t, h):
        for way in range(2):
            y_in(way, t, h)
            if t < 3:
                y_out(way, t + 1, h).start()
        if t == 3:
            y4_out(h).start()

    mate = 1 - odd

    def v_out(way, t, p):
        span = span_of(ring(r, -signs[way] * (t - 1), n_row), p, piece)
        src = lhs.at[mate, pl.ds(p * piece, piece)] if t == 1 else panel2.at[span]
        return remote(
            src, panel2.at[span], v_send.at[way, t - 1, p], v_recv.at[way, t - 1, p],
            at_row(signs[way]),
        )

    def v_in(way, t, p):
        span = span_of(ring(r, -signs[way] * t, n_row), p, piece)
        remote(
            panel2.at[span], panel2.at[span], v_send.at[way, t - 1, p],
            v_recv.at[way, t - 1, p], at_row(signs[way]),
        ).wait_recv()

    def v4_copy(p, owner):
        span = span_of(owner, p, piece)
        return remote(
            panel2.at[span], panel2.at[span], v4_send.at[p], v4_recv.at[p], at_row(side)
        )

    def v4_out(p):
        return v4_copy(p, ring(r, -3 * side, n_row))

    def v_first(p):
        for way in range(2):
            v_out(way, 1, p).start()

    def v_step(t, p):
        for way in range(2):
            v_in(way, t, p)
            if t < 3:
                v_out(way, t + 1, p).start()
        if t == 3:
            v4_out(p).start()

    def z_copy(way, t, p):
        span = pl.ds(p * piece, piece)
        src = own_ref.at[span] if t == 1 else lhs.at[2 * t - 4 + way, span]
        return remote(
            src, lhs.at[2 * t - 2 + way, span],
            z_send.at[way, t - 1, p], z_recv.at[way, t - 1, p], at_col(signs[way]),
        )

    def z_first(p):
        for way in range(2):
            z_copy(way, 1, p).start()

    def z_step(t, p):
        for way in range(2):
            z_copy(way, t, p).wait_recv()
            if t < REACH:
                z_copy(way, t + 1, p).start()

    for h in range(2):
        for way in range(2):
            y_out(way, 1, h).start()
        z_first(h)
    panel[zero_block] = jnp.zeros((panel.shape[1], panel.shape[2]), BF16)
    panel2[zero_block] = jnp.zeros((panel.shape[1], panel.shape[2]), BF16)

    nb = meta.shape[0]
    partner = c + 1 - 2 * odd
    opposite = ring(c, far, n_col)
    visitor = ring(partner, far, n_col)
    pick_copy = pltpu.make_async_copy(pick_v, pick, local_sem.at[1])
    home_copy = pltpu.make_async_copy(home_v, home, local_sem.at[2])
    table = {}

    def index_targets():
        pattern_copy.wait()
        place_copy.wait()
        pad = jnp.zeros((128 - entries - 1, nb), jnp.int32)
        meta[...] = jnp.transpose(
            jnp.concatenate([pattern_v[...], place_v[...], pad], axis=0)
        )[:, : meta.shape[1]]
        lane_of = lax.broadcasted_iota(jnp.int32, (group, lanes), 1) % group
        lane_row = jnp.where(
            lane_of // rd == opposite, lane_of + (visitor - opposite) * rd, lane_of
        )
        pick_row = lax.broadcasted_iota(jnp.int32, (group, lanes), 0) == lane_row
        mine = meta[pl.ds(pl.multiple_of(r * group, group), group), :]
        cols = [
            jnp.sum(jnp.where(pick_row, mine[:, x : x + 1], 0), axis=0, keepdims=True)
            for x in range(entries)
        ]
        lane = lax.broadcasted_iota(jnp.int32, (1, lanes), 1)
        rank = lane // group
        wanted = jnp.where((lane % group) // rd == opposite, partner, c)
        target = jnp.full((1, lanes), -1, jnp.int32)
        seen = jnp.zeros((1, lanes), jnp.int32)
        for x in range(entries):
            hit = lax.rem(cols[x], n_col) == wanted
            target = jnp.where(hit & (seen == rank), cols[x], target)
            seen = seen + hit.astype(jnp.int32)
        ids = lax.broadcasted_iota(jnp.int32, (nb, lanes), 0)
        table["slot"] = jnp.sum(
            jnp.where(ids == target, meta[:, entries : entries + 1], 0), axis=0, keepdims=True
        )
        table["cols"], table["target"] = cols, target
        table["found"] = [jnp.full((1, lanes), zero_block, jnp.int32) for _ in cols]

    def index_matches(low, high):
        slot, cols, target = table["slot"], table["cols"], table["target"]
        at_slot = lax.broadcasted_iota(jnp.int32, (nb, lanes), 0) == slot
        base = (slot // group * rd + lax.rem(slot, rd)) * entries
        for y in range(low, high):
            far_col = jnp.sum(
                jnp.where(at_slot, meta[:, y : y + 1], 0), axis=0, keepdims=True
            )
            table["found"] = [
                jnp.where((cols[x] == far_col) & (target >= 0), base + y, table["found"][x])
                for x in range(entries)
            ]

    def index_home():
        for x in range(entries):
            pick_v[pl.ds(x, 1), :] = table["found"][x]
        own_rows = meta[pl.ds(pl.multiple_of((r * n_col + c) * rd, rd), rd), :]
        width = own_rows.shape[1]
        kind = lax.rem(own_rows, n_col)
        entry = lax.broadcasted_iota(jnp.int32, (rd, width), 1)
        before = jnp.zeros((rd, width), jnp.int32)
        for x in range(entries):
            before = before + ((kind == kind[:, x : x + 1]) & (entry > x)).astype(jnp.int32)
        row = lax.broadcasted_iota(jnp.int32, (rd, width), 0)
        home_v[:, pl.ds(0, width)] = kind * unit + row * cap + before
        pick_copy.start()
        home_copy.start()

    index_steps = (
        index_targets,
        lambda: index_matches(0, entries // 2),
        lambda: index_matches(entries // 2, entries),
        index_home,
    )

    def offset(u):
        t = (u + 1) // 2
        return 0 if u == 0 else (far if t == far else (-t if u % 2 == 1 else t))

    quarter = panel.shape[1]
    rows_h = rd // 2
    blocks_h = unit // 2

    def multiply(u, h):
        source = ring(c, offset(u), n_col)
        source_panel = panel if u < n_col - 1 else panel2

        def one_row(w, carry):
            n = source * rd + w
            if u == 0:
                left = panel[pl.ds(r * shard + w * entries, entries)]
            elif u < n_col - 1:
                left = lhs[u - 1, pl.ds(w * entries, entries)]
            else:
                left = lhs[2 * REACH - 2 + odd, pl.ds(w * entries, entries)]
            left = left.reshape(entries * quarter, left.shape[2])
            right = jnp.concatenate(
                [
                    jnp.concatenate(
                        [source_panel[pick[x, m * group + n]] for x in range(entries)], axis=0
                    )
                    for m in range(cap)
                ],
                axis=1,
            )
            product = lax.dot_general(
                left, right, (((0,), (0,)), ((), ())), preferred_element_type=F32
            ).astype(BF16)
            width = left.shape[1]
            for q in range(n_depth):
                for m in range(cap):
                    part[u, q, w * cap + m] = product[
                        q * quarter : (q + 1) * quarter, m * width : (m + 1) * width
                    ]
            return carry

        lax.fori_loop(h * rows_h, (h + 1) * rows_h, one_row, 0, unroll=True)

    mid = blocks_h // 2

    def mids(h, way):
        return pl.ds(h * blocks_h + way * mid, mid)

    def half_copy(u, h, way):
        return remote(
            part.at[u, ring(d, 2, n_depth), mids(h, way)], half_in.at[u, mids(h, way)],
            h_send.at[u, h, way], h_recv.at[u, h, way], at_depth(signs[way]),
        )

    def full_copy(u, h, way):
        span = pl.ds(h * blocks_h, blocks_h)
        return remote(
            part.at[u, ring(d, signs[way], n_depth), span], full_in.at[u, way, span],
            f_send.at[u, h, way], f_recv.at[u, h, way], at_depth(signs[way]),
        )

    def shift(u):
        return 2 * REACH * odd - REACH if u == n_col - 1 else offset(u)

    def back_copy(u, h, kind_of):
        span = pl.ds(kind_of * unit + h * blocks_h, blocks_h)
        return remote(
            part.at[u, d, pl.ds(h * blocks_h, blocks_h)], back.at[span],
            b_send.at[u, h], b_recv.at[u, h], at_col(shift(u)),
        )

    def back_out(u, h):
        return back_copy(u, h, partner if u == n_col - 1 else c)

    def first(u, h):
        for way in range(2):
            half_copy(u, h, way).start()

    def second(u, h):
        for way in range(2):
            half_copy(u, h, way).wait_recv()
            q = ring(d, signs[way], n_depth)
            total = part[u, q, mids(h, way)].astype(F32) + half_in[u, mids(h, way)].astype(F32)
            part[u, q, mids(h, way)] = total.astype(BF16)
            full_copy(u, h, way).start()

    def third(u, h):
        for way in range(2):
            full_copy(u, h, way).wait_recv()
        span = pl.ds(h * blocks_h, blocks_h)
        total = (
            part[u, d, span].astype(F32)
            + full_in[u, 0, span].astype(F32)
            + full_in[u, 1, span].astype(F32)
        ).astype(BF16)
        if u == 0:
            back[pl.ds(c * unit + h * blocks_h, blocks_h)] = total
        else:
            part[u, d, span] = total

    mate_copy = pltpu.make_async_copy(
        lhs.at[mate], panel2.at[pl.ds(r * shard, shard)], local_sem.at[5]
    )
    here = []

    def z_event(t, p):
        z_step(t, p)
        if t == 1:
            here.append(p)
            if len(here) == PIECES:
                mate_copy.start()

    def whole_panel():
        own_copy.wait()
        pick_copy.wait()
        home_copy.wait()
        for h in range(2):
            y4_copy(h, ring(r, 4, n_row)).wait_recv()

    def whole_panel2():
        mate_copy.wait()
        for p in range(PIECES):
            v4_copy(p, ring(r, 4, n_row)).wait_recv()

    def mul(u, h):
        multiply(u, h)
        first(u, h)

    steps = {
        "y": y_step, "z": z_event, "zf": z_first, "v": v_step, "vf": v_first,
        "index": lambda k: index_steps[k](), "panel": whole_panel, "panel2": whole_panel2,
        "mul": mul, "add": second, "end": third,
        "give": lambda u, h: back_out(u, h).start(),
    }
    for step in ORDER:
        steps[step[0]](*step[1:])

    for way in range(2):
        for t in range(1, REACH + 1):
            for h in range(2):
                y_out(way, t, h).wait_send()
            for p in range(PIECES):
                z_copy(way, t, p).wait_send()
                v_out(way, t, p).wait_send()
        for u in range(n_col):
            for h in range(2):
                half_copy(u, h, way).wait_send()
                full_copy(u, h, way).wait_send()
    for h in range(2):
        y4_out(h).wait_send()
        for u in range(1, n_col):
            back_out(u, h).wait_send()
    for p in range(PIECES):
        v4_out(p).wait_send()

    for u in range(1, n_col):
        for h in range(2):
            kind_of = ring(c, -offset(u), n_col)
            back_copy(u, h, kind_of).wait_recv()
    for w in range(rd):
        for a in range(entries):
            out_ref[w * entries + a] = back[home[w, a]]


def solution(mesh):
    n_row, n_col, n_depth = mesh.shape["row"], mesh.shape["col"], mesh.shape["depth"]

    def body(blocks, pattern, place):
        rd, entries, quarter, width = blocks.shape
        nb = pattern.shape[0]
        cap = (entries + n_col - 1) // n_col
        shard, unit = rd * entries, rd * cap
        lanes = cap * rd * n_col
        dma, vmem, ints = pltpu.SemaphoreType.DMA, pltpu.VMEM, jnp.int32
        result = pl.pallas_call(
            functools.partial(kernel, n_row, n_col, n_depth, rd, entries, cap),
            out_shape=jax.ShapeDtypeStruct((shard, quarter, width), BF16),
            in_specs=[pl.BlockSpec(memory_space=pltpu.HBM)] * 3,
            out_specs=pl.BlockSpec(memory_space=pltpu.VMEM),
            scratch_shapes=[
                vmem((n_row * shard + 1, quarter, width), BF16),
                vmem((n_row * shard + 1, quarter, width), BF16),
                vmem((2 * REACH, shard, quarter, width), BF16),
                vmem((n_col, n_depth, unit, quarter, width), BF16),
                vmem((n_col, unit, quarter, width), BF16),
                vmem((n_col, 2, unit, quarter, width), BF16),
                vmem((n_col * unit, quarter, width), BF16),
                vmem((entries, nb), ints), vmem((1, nb), ints), vmem((nb, 16), ints),
                vmem((16, lanes), ints), vmem((8, 128), ints),
                pltpu.SMEM((16, lanes), ints), pltpu.SMEM((8, 128), ints),
                dma((2, 3, 2)), dma((2, 3, 2)), dma((2,)), dma((2,)),
                dma((2, REACH, PIECES)), dma((2, REACH, PIECES)),
                dma((2, 3, PIECES)), dma((2, 3, PIECES)), dma((PIECES,)), dma((PIECES,)),
                dma((n_col, 2, 2)), dma((n_col, 2, 2)),
                dma((n_col, 2, 2)), dma((n_col, 2, 2)),
                dma((n_col, 2)), dma((n_col, 2)),
                dma((6,)),
            ],
            compiler_params=pltpu.CompilerParams(
                collective_id=0, has_side_effects=True, vmem_limit_bytes=62 * 2**20
            ),
        )(blocks.reshape(shard, quarter, width), pattern.T, place.reshape(1, nb))
        return result.reshape(blocks.shape)

    placed = (P(("row", "col"), None, "depth", None), P(), P())
    return jax.shard_map(
        body,
        mesh=mesh,
        in_specs=placed,
        out_specs=P(("row", "col"), None, "depth", None),
        check_vma=False,
    )
```

```python
import functools

import jax
import jax.numpy as jnp
from jax import lax
from jax.experimental import pallas as pl
from jax.experimental.pallas import tpu as pltpu
from jax.sharding import PartitionSpec as P

MESH = pl.DeviceIdType.MESH
F32 = jnp.float32
BF16 = jnp.bfloat16
REACH = 3
PIECES = 4

ORDER = (
    ("index", 0), ("index", 1), ("index", 2), ("index", 3), ("y", 1, 0), ("z", 1, 0),
    ("y", 1, 1), ("z", 1, 1), ("y", 2, 0), ("z", 2, 0), ("zf", 2), ("y", 2, 1), ("z", 2, 1),
    ("zf", 3), ("y", 3, 0), ("z", 3, 0), ("vf", 0), ("vf", 1), ("y", 3, 1), ("z", 1, 2),
    ("panel",), ("mul", 1, 0), ("v", 1, 0), ("mul", 2, 0), ("mul", 3, 0), ("mul", 4, 0),
    ("mul", 0, 0), ("mul", 0, 1), ("z", 3, 1), ("v", 1, 1), ("add", 1, 0), ("mul", 5, 0),
    ("add", 2, 0), ("add", 3, 0), ("v", 2, 0), ("add", 4, 0), ("add", 0, 0), ("add", 0, 1),
    ("z", 1, 3), ("v", 2, 1), ("end", 1, 0), ("mul", 6, 0), ("add", 5, 0), ("mul", 1, 1),
    ("mul", 2, 1), ("v", 3, 0), ("vf", 2), ("vf", 3), ("end", 2, 0), ("end", 3, 0),
    ("z", 2, 2), ("v", 3, 1), ("end", 4, 0), ("end", 0, 0), ("v", 1, 2), ("end", 0, 1),
    ("z", 2, 3), ("add", 6, 0), ("give", 1, 0), ("give", 2, 0), ("give", 3, 0), ("give", 4, 0),
    ("mul", 3, 1), ("v", 1, 3), ("end", 5, 0), ("add", 1, 1), ("add", 2, 1), ("give", 5, 0),
    ("mul", 4, 1), ("v", 2, 2), ("end", 6, 0), ("z", 3, 2), ("give", 6, 0), ("add", 3, 1),
    ("v", 2, 3), ("end", 1, 1), ("give", 1, 1), ("end", 2, 1), ("give", 2, 1), ("add", 4, 1),
    ("v", 3, 2), ("z", 3, 3), ("mul", 5, 1), ("mul", 6, 1), ("end", 3, 1), ("give", 3, 1),
    ("v", 3, 3), ("end", 4, 1), ("give", 4, 1), ("panel2",), ("mul", 7, 0), ("mul", 7, 1),
    ("add", 5, 1), ("add", 6, 1), ("add", 7, 0), ("add", 7, 1), ("end", 5, 1), ("give", 5, 1),
    ("end", 6, 1), ("give", 6, 1), ("end", 7, 0), ("give", 7, 0), ("end", 7, 1),
    ("give", 7, 1),
)


def kernel(
    n_row, n_col, n_depth, rd, entries, cap,
    own_ref, pattern_ref, place_ref, out_ref,
    panel, panel2, lhs, part, half_in, full_in, back,
    pattern_v, place_v, meta, pick_v, home_v, pick, home,
    y_send, y_recv, y4_send, y4_recv, z_send, z_recv,
    v_send, v_recv, v4_send, v4_recv,
    h_send, h_recv, f_send, f_recv, b_send, b_recv, local_sem,
):
    r, c, d = lax.axis_index("row"), lax.axis_index("col"), lax.axis_index("depth")
    core, odd = lax.rem(r, 2), lax.rem(c, 2)
    shard = rd * entries
    piece = shard // PIECES
    half = shard // 2
    group = rd * n_col
    lanes = cap * group
    zero_block = n_row * shard
    unit = rd * cap
    far = n_col // 2

    def ring(me, step, size):
        return lax.rem(me + step + size, size)

    def at_row(step):
        return (ring(r, step, n_row), c, d)

    def at_col(step):
        return (r, ring(c, step, n_col), d)

    def at_depth(step):
        return (r, c, ring(d, step, n_depth))

    def remote(src, dst, send, recv, to):
        return pltpu.make_async_remote_copy(
            src_ref=src, dst_ref=dst, send_sem=send, recv_sem=recv,
            device_id=to, device_id_type=MESH,
        )

    partners = [at_row(1), at_row(-1), at_depth(1), at_depth(-1)]
    partners += [at_col(1), at_col(-1)]
    pattern_copy = pltpu.make_async_copy(pattern_ref, pattern_v, local_sem.at[3])
    place_copy = pltpu.make_async_copy(place_ref, place_v, local_sem.at[4])
    own_copy = pltpu.make_async_copy(
        own_ref, panel.at[pl.ds(r * shard, shard)], local_sem.at[0]
    )
    pattern_copy.start()
    place_copy.start()
    own_copy.start()
    barrier = pltpu.get_barrier_semaphore()
    for other in partners:
        pl.semaphore_signal(barrier, inc=1, device_id=other, device_id_type=MESH)
    pl.semaphore_wait(barrier, len(partners))

    signs = (1, -1)
    side = 1 - 2 * core

    def span_of(owner, p, size):
        return pl.ds(owner * shard + p * size, size)

    def y_copy(way, t, h, owner_step):
        span = span_of(ring(r, owner_step, n_row), h, half)
        src = own_ref.at[pl.ds(h * half, half)] if t == 1 else panel.at[span]
        return remote(
            src, panel.at[span], y_send.at[way, t - 1, h], y_recv.at[way, t - 1, h],
            at_row(signs[way]),
        )

    def y_out(way, t, h):
        return y_copy(way, t, h, -signs[way] * (t - 1))

    def y_in(way, t, h):
        span = span_of(ring(r, -signs[way] * t, n_row), h, half)
        remote(
            panel.at[span], panel.at[span], y_send.at[way, t - 1, h],
            y_recv.at[way, t - 1, h], at_row(signs[way]),
        ).wait_recv()

    def y4_copy(h, owner):
        span = span_of(owner, h, half)
        return remote(
            panel.at[span], panel.at[span], y4_send.at[h], y4_recv.at[h], at_row(side)
        )

    def y4_out(h):
        return y4_copy(h, ring(r, -3 * side, n_row))

    def y_step(t, h):
        for way in range(2):
            y_in(way, t, h)
            if t < 3:
                y_out(way, t + 1, h).start()
        if t == 3:
            y4_out(h).start()

    mate = 1 - odd

    def v_out(way, t, p):
        span = span_of(ring(r, -signs[way] * (t - 1), n_row), p, piece)
        src = lhs.at[mate, pl.ds(p * piece, piece)] if t == 1 else panel2.at[span]
        return remote(
            src, panel2.at[span], v_send.at[way, t - 1, p], v_recv.at[way, t - 1, p],
            at_row(signs[way]),
        )

    def v_in(way, t, p):
        span = span_of(ring(r, -signs[way] * t, n_row), p, piece)
        remote(
            panel2.at[span], panel2.at[span], v_send.at[way, t - 1, p],
            v_recv.at[way, t - 1, p], at_row(signs[way]),
        ).wait_recv()

    def v4_copy(p, owner):
        span = span_of(owner, p, piece)
        return remote(
            panel2.at[span], panel2.at[span], v4_send.at[p], v4_recv.at[p], at_row(side)
        )

    def v4_out(p):
        return v4_copy(p, ring(r, -3 * side, n_row))

    def v_first(p):
        for way in range(2):
            v_out(way, 1, p).start()

    def v_step(t, p):
        for way in range(2):
            v_in(way, t, p)
            if t < 3:
                v_out(way, t + 1, p).start()
        if t == 3:
            v4_out(p).start()

    def z_copy(way, t, p):
        span = pl.ds(p * piece, piece)
        src = own_ref.at[span] if t == 1 else lhs.at[2 * t - 4 + way, span]
        return remote(
            src, lhs.at[2 * t - 2 + way, span],
            z_send.at[way, t - 1, p], z_recv.at[way, t - 1, p], at_col(signs[way]),
        )

    def z_first(p):
        for way in range(2):
            z_copy(way, 1, p).start()

    def z_step(t, p):
        for way in range(2):
            z_copy(way, t, p).wait_recv()
            if t < REACH:
                z_copy(way, t + 1, p).start()

    for h in range(2):
        for way in range(2):
            y_out(way, 1, h).start()
        z_first(h)
    panel[zero_block] = jnp.zeros((panel.shape[1], panel.shape[2]), BF16)
    panel2[zero_block] = jnp.zeros((panel.shape[1], panel.shape[2]), BF16)

    nb = meta.shape[0]
    partner = c + 1 - 2 * odd
    opposite = ring(c, far, n_col)
    visitor = ring(partner, far, n_col)
    pick_copy = pltpu.make_async_copy(pick_v, pick, local_sem.at[1])
    home_copy = pltpu.make_async_copy(home_v, home, local_sem.at[2])
    table = {}

    def index_targets():
        pattern_copy.wait()
        place_copy.wait()
        pad = jnp.zeros((128 - entries - 1, nb), jnp.int32)
        meta[...] = jnp.transpose(
            jnp.concatenate([pattern_v[...], place_v[...], pad], axis=0)
        )[:, : meta.shape[1]]
        lane_of = lax.broadcasted_iota(jnp.int32, (group, lanes), 1) % group
        lane_row = jnp.where(
            lane_of // rd == opposite, lane_of + (visitor - opposite) * rd, lane_of
        )
        pick_row = lax.broadcasted_iota(jnp.int32, (group, lanes), 0) == lane_row
        mine = meta[pl.ds(pl.multiple_of(r * group, group), group), :]
        cols = [
            jnp.sum(jnp.where(pick_row, mine[:, x : x + 1], 0), axis=0, keepdims=True)
            for x in range(entries)
        ]
        lane = lax.broadcasted_iota(jnp.int32, (1, lanes), 1)
        rank = lane // group
        wanted = jnp.where((lane % group) // rd == opposite, partner, c)
        target = jnp.full((1, lanes), -1, jnp.int32)
        seen = jnp.zeros((1, lanes), jnp.int32)
        for x in range(entries):
            hit = lax.rem(cols[x], n_col) == wanted
            target = jnp.where(hit & (seen == rank), cols[x], target)
            seen = seen + hit.astype(jnp.int32)
        ids = lax.broadcasted_iota(jnp.int32, (nb, lanes), 0)
        table["slot"] = jnp.sum(
            jnp.where(ids == target, meta[:, entries : entries + 1], 0), axis=0, keepdims=True
        )
        table["cols"], table["target"] = cols, target
        table["found"] = [jnp.full((1, lanes), zero_block, jnp.int32) for _ in cols]

    def index_matches(low, high):
        slot, cols, target = table["slot"], table["cols"], table["target"]
        at_slot = lax.broadcasted_iota(jnp.int32, (nb, lanes), 0) == slot
        base = (slot // group * rd + lax.rem(slot, rd)) * entries
        for y in range(low, high):
            far_col = jnp.sum(
                jnp.where(at_slot, meta[:, y : y + 1], 0), axis=0, keepdims=True
            )
            table["found"] = [
                jnp.where((cols[x] == far_col) & (target >= 0), base + y, table["found"][x])
                for x in range(entries)
            ]

    def index_home():
        for x in range(entries):
            pick_v[pl.ds(x, 1), :] = table["found"][x]
        own_rows = meta[pl.ds(pl.multiple_of((r * n_col + c) * rd, rd), rd), :]
        width = own_rows.shape[1]
        kind = lax.rem(own_rows, n_col)
        entry = lax.broadcasted_iota(jnp.int32, (rd, width), 1)
        before = jnp.zeros((rd, width), jnp.int32)
        for x in range(entries):
            before = before + ((kind == kind[:, x : x + 1]) & (entry > x)).astype(jnp.int32)
        row = lax.broadcasted_iota(jnp.int32, (rd, width), 0)
        home_v[:, pl.ds(0, width)] = kind * unit + row * cap + before
        pick_copy.start()
        home_copy.start()

    index_steps = (
        index_targets,
        lambda: index_matches(0, entries // 2),
        lambda: index_matches(entries // 2, entries),
        index_home,
    )

    def offset(u):
        t = (u + 1) // 2
        return 0 if u == 0 else (far if t == far else (-t if u % 2 == 1 else t))

    quarter = panel.shape[1]
    rows_h = rd // 2
    blocks_h = unit // 2

    def multiply(u, h):
        source = ring(c, offset(u), n_col)
        source_panel = panel if u < n_col - 1 else panel2

        def one_row(w, carry):
            n = source * rd + w
            if u == 0:
                left = panel[pl.ds(r * shard + w * entries, entries)]
            elif u < n_col - 1:
                left = lhs[u - 1, pl.ds(w * entries, entries)]
            else:
                left = lhs[2 * REACH - 2 + odd, pl.ds(w * entries, entries)]
            left = left.reshape(entries * quarter, left.shape[2])
            right = jnp.concatenate(
                [
                    jnp.concatenate(
                        [source_panel[pick[x, m * group + n]] for x in range(entries)], axis=0
                    )
                    for m in range(cap)
                ],
                axis=1,
            )
            product = lax.dot_general(
                left, right, (((0,), (0,)), ((), ())), preferred_element_type=F32
            ).astype(BF16)
            width = left.shape[1]
            for q in range(n_depth):
                for m in range(cap):
                    part[u, q, w * cap + m] = product[
                        q * quarter : (q + 1) * quarter, m * width : (m + 1) * width
                    ]
            return carry

        lax.fori_loop(h * rows_h, (h + 1) * rows_h, one_row, 0, unroll=True)

    mid = blocks_h // 2

    def mids(h, way):
        return pl.ds(h * blocks_h + way * mid, mid)

    def half_copy(u, h, way):
        return remote(
            part.at[u, ring(d, 2, n_depth), mids(h, way)], half_in.at[u, mids(h, way)],
            h_send.at[u, h, way], h_recv.at[u, h, way], at_depth(signs[way]),
        )

    def full_copy(u, h, way):
        span = pl.ds(h * blocks_h, blocks_h)
        return remote(
            part.at[u, ring(d, signs[way], n_depth), span], full_in.at[u, way, span],
            f_send.at[u, h, way], f_recv.at[u, h, way], at_depth(signs[way]),
        )

    def shift(u):
        return 2 * REACH * odd - REACH if u == n_col - 1 else offset(u)

    def back_copy(u, h, kind_of):
        span = pl.ds(kind_of * unit + h * blocks_h, blocks_h)
        return remote(
            part.at[u, d, pl.ds(h * blocks_h, blocks_h)], back.at[span],
            b_send.at[u, h], b_recv.at[u, h], at_col(shift(u)),
        )

    def back_out(u, h):
        return back_copy(u, h, partner if u == n_col - 1 else c)

    def first(u, h):
        for way in range(2):
            half_copy(u, h, way).start()

    def second(u, h):
        for way in range(2):
            half_copy(u, h, way).wait_recv()
            q = ring(d, signs[way], n_depth)
            total = part[u, q, mids(h, way)].astype(F32) + half_in[u, mids(h, way)].astype(F32)
            part[u, q, mids(h, way)] = total.astype(BF16)
            full_copy(u, h, way).start()

    def third(u, h):
        for way in range(2):
            full_copy(u, h, way).wait_recv()
        span = pl.ds(h * blocks_h, blocks_h)
        total = (
            part[u, d, span].astype(F32)
            + full_in[u, 0, span].astype(F32)
            + full_in[u, 1, span].astype(F32)
        ).astype(BF16)
        if u == 0:
            back[pl.ds(c * unit + h * blocks_h, blocks_h)] = total
        else:
            part[u, d, span] = total

    mate_copy = pltpu.make_async_copy(
        lhs.at[mate], panel2.at[pl.ds(r * shard, shard)], local_sem.at[5]
    )
    here = []

    def z_event(t, p):
        z_step(t, p)
        if t == 1:
            here.append(p)
            if len(here) == PIECES:
                mate_copy.start()

    def whole_panel():
        own_copy.wait()
        pick_copy.wait()
        home_copy.wait()
        for h in range(2):
            y4_copy(h, ring(r, 4, n_row)).wait_recv()

    def whole_panel2():
        mate_copy.wait()
        for p in range(PIECES):
            v4_copy(p, ring(r, 4, n_row)).wait_recv()

    def mul(u, h):
        multiply(u, h)
        first(u, h)

    steps = {
        "y": y_step, "z": z_event, "zf": z_first, "v": v_step, "vf": v_first,
        "index": lambda k: index_steps[k](), "panel": whole_panel, "panel2": whole_panel2,
        "mul": mul, "add": second, "end": third,
        "give": lambda u, h: back_out(u, h).start(),
    }
    for step in ORDER:
        steps[step[0]](*step[1:])

    for way in range(2):
        for t in range(1, REACH + 1):
            for h in range(2):
                y_out(way, t, h).wait_send()
            for p in range(PIECES):
                z_copy(way, t, p).wait_send()
                v_out(way, t, p).wait_send()
        for u in range(n_col):
            for h in range(2):
                half_copy(u, h, way).wait_send()
                full_copy(u, h, way).wait_send()
    for h in range(2):
        y4_out(h).wait_send()
        for u in range(1, n_col):
            back_out(u, h).wait_send()
    for p in range(PIECES):
        v4_out(p).wait_send()

    for u in range(1, n_col):
        for h in range(2):
            kind_of = ring(c, -offset(u), n_col)
            back_copy(u, h, kind_of).wait_recv()
    for w in range(rd):
        for a in range(entries):
            out_ref[w * entries + a] = back[home[w, a]]


def solution(mesh):
    n_row, n_col, n_depth = mesh.shape["row"], mesh.shape["col"], mesh.shape["depth"]

    def body(blocks, pattern, place):
        rd, entries, quarter, width = blocks.shape
        nb = pattern.shape[0]
        cap = (entries + n_col - 1) // n_col
        shard, unit = rd * entries, rd * cap
        lanes = cap * rd * n_col
        dma, vmem, ints = pltpu.SemaphoreType.DMA, pltpu.VMEM, jnp.int32
        result = pl.pallas_call(
            functools.partial(kernel, n_row, n_col, n_depth, rd, entries, cap),
            out_shape=jax.ShapeDtypeStruct((shard, quarter, width), BF16),
            in_specs=[pl.BlockSpec(memory_space=pltpu.HBM)] * 3,
            out_specs=pl.BlockSpec(memory_space=pltpu.VMEM),
            scratch_shapes=[
                vmem((n_row * shard + 1, quarter, width), BF16),
                vmem((n_row * shard + 1, quarter, width), BF16),
                vmem((2 * REACH, shard, quarter, width), BF16),
                vmem((n_col, n_depth, unit, quarter, width), BF16),
                vmem((n_col, unit, quarter, width), BF16),
                vmem((n_col, 2, unit, quarter, width), BF16),
                vmem((n_col * unit, quarter, width), BF16),
                vmem((entries, nb), ints), vmem((1, nb), ints), vmem((nb, 16), ints),
                vmem((16, lanes), ints), vmem((8, 128), ints),
                pltpu.SMEM((16, lanes), ints), pltpu.SMEM((8, 128), ints),
                dma((2, 3, 2)), dma((2, 3, 2)), dma((2,)), dma((2,)),
                dma((2, REACH, PIECES)), dma((2, REACH, PIECES)),
                dma((2, 3, PIECES)), dma((2, 3, PIECES)), dma((PIECES,)), dma((PIECES,)),
                dma((n_col, 2, 2)), dma((n_col, 2, 2)),
                dma((n_col, 2, 2)), dma((n_col, 2, 2)),
                dma((n_col, 2)), dma((n_col, 2)),
                dma((6,)),
            ],
            compiler_params=pltpu.CompilerParams(
                collective_id=0, has_side_effects=True, vmem_limit_bytes=48 * 2**20
            ),
        )(*(
            pltpu.with_memory_space_constraint(x, pltpu.HBM)
            for x in (blocks.reshape(shard, quarter, width), pattern.T, place.reshape(1, nb))
        ))
        return result.reshape(blocks.shape)

    placed = (P(("row", "col"), None, "depth", None), P(), P())
    return jax.shard_map(
        body,
        mesh=mesh,
        in_specs=placed,
        out_specs=P(("row", "col"), None, "depth", None),
        check_vma=False,
    )
```

```python
import functools

import jax
import jax.numpy as jnp
from jax import lax
from jax.experimental import pallas as pl
from jax.experimental.pallas import tpu as pltpu
from jax.sharding import PartitionSpec as P

MESH = pl.DeviceIdType.MESH
F32 = jnp.float32
BF16 = jnp.bfloat16
REACH = 3
PIECES = 4

ORDER = (
    ("index", 0), ("index", 1), ("index", 2), ("index", 3), ("y", 1, 0), ("z", 1, 0),
    ("y", 1, 1), ("z", 1, 1), ("y", 2, 0), ("z", 1, 2), ("y", 2, 1), ("z", 1, 3), ("y", 3, 0),
    ("z", 2, 0), ("vf", 0), ("y", 3, 1), ("z", 2, 1), ("vf", 1), ("panel",), ("mul", 1, 0),
    ("v", 1, 0), ("mul", 2, 0), ("mul", 3, 0), ("mul", 4, 0), ("mul", 1, 1), ("mul", 2, 1),
    ("z", 2, 2), ("v", 1, 1), ("add", 1, 0), ("add", 2, 0), ("mul", 0, 0), ("add", 3, 0),
    ("v", 2, 0), ("add", 4, 0), ("add", 1, 1), ("add", 2, 1), ("z", 2, 3), ("v", 2, 1),
    ("end", 1, 0), ("give", 1, 0), ("mul", 3, 1), ("mul", 4, 1), ("end", 2, 0), ("give", 2, 0),
    ("add", 0, 0), ("v", 3, 0), ("vf", 2), ("vf", 3), ("mul", 0, 1), ("z", 3, 0),
    ("end", 3, 0), ("give", 3, 0), ("v", 3, 1), ("end", 4, 0), ("give", 4, 0), ("end", 1, 1),
    ("give", 1, 1), ("end", 2, 1), ("v", 1, 2), ("z", 3, 1), ("add", 3, 1), ("add", 4, 1),
    ("give", 2, 1), ("mul", 5, 0), ("v", 1, 3), ("end", 0, 0), ("mul", 6, 0), ("add", 0, 1),
    ("end", 3, 1), ("z", 3, 2), ("v", 2, 2), ("give", 3, 1), ("end", 4, 1), ("give", 4, 1),
    ("add", 5, 0), ("v", 2, 3), ("add", 6, 0), ("end", 0, 1), ("z", 3, 3), ("mul", 5, 1),
    ("v", 3, 2), ("mul", 6, 1), ("end", 5, 0), ("give", 5, 0), ("end", 6, 0), ("v", 3, 3),
    ("give", 6, 0), ("add", 5, 1), ("add", 6, 1), ("panel2",), ("mul", 7, 0), ("mul", 7, 1),
    ("end", 5, 1), ("give", 5, 1), ("end", 6, 1), ("give", 6, 1), ("add", 7, 0), ("add", 7, 1),
    ("end", 7, 0), ("give", 7, 0), ("end", 7, 1), ("give", 7, 1),
)


def kernel(
    n_row, n_col, n_depth, rd, entries, cap,
    own_ref, pattern_ref, place_ref, out_ref,
    panel, panel2, lhs, part, half_in, full_in, back,
    pattern_v, place_v, meta, pick_v, home_v, pick, home,
    y_send, y_recv, y4_send, y4_recv, z_send, z_recv,
    v_send, v_recv, v4_send, v4_recv,
    h_send, h_recv, f_send, f_recv, b_send, b_recv, local_sem,
):
    r, c, d = lax.axis_index("row"), lax.axis_index("col"), lax.axis_index("depth")
    core, odd = lax.rem(r, 2), lax.rem(c + 2, 4) // 2
    shard = rd * entries
    piece = shard // PIECES
    half = shard // 2
    group = rd * n_col
    lanes = cap * group
    zero_block = n_row * shard
    unit = rd * cap
    far = n_col // 2

    def ring(me, step, size):
        return lax.rem(me + step + size, size)

    def at_row(step):
        return (ring(r, step, n_row), c, d)

    def at_col(step):
        return (r, ring(c, step, n_col), d)

    def at_depth(step):
        return (r, c, ring(d, step, n_depth))

    def remote(src, dst, send, recv, to):
        return pltpu.make_async_remote_copy(
            src_ref=src, dst_ref=dst, send_sem=send, recv_sem=recv,
            device_id=to, device_id_type=MESH,
        )

    partners = [at_row(1), at_row(-1), at_depth(1), at_depth(-1)]
    partners += [at_col(1), at_col(-1)]
    pattern_copy = pltpu.make_async_copy(pattern_ref, pattern_v, local_sem.at[3])
    place_copy = pltpu.make_async_copy(place_ref, place_v, local_sem.at[4])
    own_copy = pltpu.make_async_copy(
        own_ref, panel.at[pl.ds(r * shard, shard)], local_sem.at[0]
    )
    barrier = pltpu.get_barrier_semaphore()
    for other in partners:
        pl.semaphore_signal(barrier, inc=1, device_id=other, device_id_type=MESH)
    pl.semaphore_wait(barrier, len(partners))

    signs = (1, -1)
    side = 1 - 2 * core

    def span_of(owner, p, size):
        return pl.ds(owner * shard + p * size, size)

    def y_copy(way, t, h, owner_step):
        span = span_of(ring(r, owner_step, n_row), h, half)
        src = own_ref.at[pl.ds(h * half, half)] if t == 1 else panel.at[span]
        return remote(
            src, panel.at[span], y_send.at[way, t - 1, h], y_recv.at[way, t - 1, h],
            at_row(signs[way]),
        )

    def y_out(way, t, h):
        return y_copy(way, t, h, -signs[way] * (t - 1))

    def y_in(way, t, h):
        span = span_of(ring(r, -signs[way] * t, n_row), h, half)
        remote(
            panel.at[span], panel.at[span], y_send.at[way, t - 1, h],
            y_recv.at[way, t - 1, h], at_row(signs[way]),
        ).wait_recv()

    def y4_copy(h, owner):
        span = span_of(owner, h, half)
        return remote(
            panel.at[span], panel.at[span], y4_send.at[h], y4_recv.at[h], at_row(side)
        )

    def y4_out(h):
        return y4_copy(h, ring(r, -3 * side, n_row))

    def y_step(t, h):
        for way in range(2):
            y_in(way, t, h)
            if t < 3:
                y_out(way, t + 1, h).start()
        if t == 3:
            y4_out(h).start()

    mate = 3 - odd

    def v_out(way, t, p):
        span = span_of(ring(r, -signs[way] * (t - 1), n_row), p, piece)
        src = lhs.at[mate, pl.ds(p * piece, piece)] if t == 1 else panel2.at[span]
        return remote(
            src, panel2.at[span], v_send.at[way, t - 1, p], v_recv.at[way, t - 1, p],
            at_row(signs[way]),
        )

    def v_in(way, t, p):
        span = span_of(ring(r, -signs[way] * t, n_row), p, piece)
        remote(
            panel2.at[span], panel2.at[span], v_send.at[way, t - 1, p],
            v_recv.at[way, t - 1, p], at_row(signs[way]),
        ).wait_recv()

    def v4_copy(p, owner):
        span = span_of(owner, p, piece)
        return remote(
            panel2.at[span], panel2.at[span], v4_send.at[p], v4_recv.at[p], at_row(side)
        )

    def v4_out(p):
        return v4_copy(p, ring(r, -3 * side, n_row))

    def v_first(p):
        for way in range(2):
            v_out(way, 1, p).start()

    def v_step(t, p):
        for way in range(2):
            v_in(way, t, p)
            if t < 3:
                v_out(way, t + 1, p).start()
        if t == 3:
            v4_out(p).start()

    def z_copy(way, t, p):
        span = pl.ds(p * piece, piece)
        src = own_ref.at[span] if t == 1 else lhs.at[2 * t - 4 + way, span]
        return remote(
            src, lhs.at[2 * t - 2 + way, span],
            z_send.at[way, t - 1, p], z_recv.at[way, t - 1, p], at_col(signs[way]),
        )

    def z_first(p):
        for way in range(2):
            z_copy(way, 1, p).start()

    def z_step(t, p):
        for way in range(2):
            z_copy(way, t, p).wait_recv()
            if t < REACH:
                z_copy(way, t + 1, p).start()

    for h in range(2):
        z_first(h)
        for way in range(2):
            y_out(way, 1, h).start()
    z_first(2)
    z_first(3)
    pattern_copy.start()
    place_copy.start()
    own_copy.start()
    panel[zero_block] = jnp.zeros((panel.shape[1], panel.shape[2]), BF16)
    panel2[zero_block] = jnp.zeros((panel.shape[1], panel.shape[2]), BF16)

    nb = meta.shape[0]
    partner = ring(c, 2 - 4 * odd, n_col)
    opposite = ring(c, far, n_col)
    visitor = ring(partner, far, n_col)
    pick_copy = pltpu.make_async_copy(pick_v, pick, local_sem.at[1])
    home_copy = pltpu.make_async_copy(home_v, home, local_sem.at[2])
    table = {}

    def index_targets():
        pattern_copy.wait()
        place_copy.wait()
        pad = jnp.zeros((128 - entries - 1, nb), jnp.int32)
        meta[...] = jnp.transpose(
            jnp.concatenate([pattern_v[...], place_v[...], pad], axis=0)
        )[:, : meta.shape[1]]
        lane_of = lax.broadcasted_iota(jnp.int32, (group, lanes), 1) % group
        lane_row = jnp.where(
            lane_of // rd == opposite, lane_of + (visitor - opposite) * rd, lane_of
        )
        pick_row = lax.broadcasted_iota(jnp.int32, (group, lanes), 0) == lane_row
        mine = meta[pl.ds(pl.multiple_of(r * group, group), group), :]
        cols = [
            jnp.sum(jnp.where(pick_row, mine[:, x : x + 1], 0), axis=0, keepdims=True)
            for x in range(entries)
        ]
        lane = lax.broadcasted_iota(jnp.int32, (1, lanes), 1)
        rank = lane // group
        wanted = jnp.where((lane % group) // rd == opposite, partner, c)
        target = jnp.full((1, lanes), -1, jnp.int32)
        seen = jnp.zeros((1, lanes), jnp.int32)
        for x in range(entries):
            hit = lax.rem(cols[x], n_col) == wanted
            target = jnp.where(hit & (seen == rank), cols[x], target)
            seen = seen + hit.astype(jnp.int32)
        ids = lax.broadcasted_iota(jnp.int32, (nb, lanes), 0)
        table["slot"] = jnp.sum(
            jnp.where(ids == target, meta[:, entries : entries + 1], 0), axis=0, keepdims=True
        )
        table["cols"], table["target"] = cols, target
        table["found"] = [jnp.full((1, lanes), zero_block, jnp.int32) for _ in cols]

    def index_matches(low, high):
        slot, cols, target = table["slot"], table["cols"], table["target"]
        at_slot = lax.broadcasted_iota(jnp.int32, (nb, lanes), 0) == slot
        base = (slot // group * rd + lax.rem(slot, rd)) * entries
        for y in range(low, high):
            far_col = jnp.sum(
                jnp.where(at_slot, meta[:, y : y + 1], 0), axis=0, keepdims=True
            )
            table["found"] = [
                jnp.where((cols[x] == far_col) & (target >= 0), base + y, table["found"][x])
                for x in range(entries)
            ]

    def index_home():
        for x in range(entries):
            pick_v[pl.ds(x, 1), :] = table["found"][x]
        own_rows = meta[pl.ds(pl.multiple_of((r * n_col + c) * rd, rd), rd), :]
        width = own_rows.shape[1]
        kind = lax.rem(own_rows, n_col)
        entry = lax.broadcasted_iota(jnp.int32, (rd, width), 1)
        before = jnp.zeros((rd, width), jnp.int32)
        for x in range(entries):
            before = before + ((kind == kind[:, x : x + 1]) & (entry > x)).astype(jnp.int32)
        row = lax.broadcasted_iota(jnp.int32, (rd, width), 0)
        home_v[:, pl.ds(0, width)] = kind * unit + row * cap + before
        pick_copy.start()
        home_copy.start()

    index_steps = (
        index_targets,
        lambda: index_matches(0, entries // 2),
        lambda: index_matches(entries // 2, entries),
        index_home,
    )

    def offset(u):
        t = (u + 1) // 2
        return 0 if u == 0 else (far if t == far else (-t if u % 2 == 1 else t))

    quarter = panel.shape[1]
    rows_h = rd // 2
    blocks_h = unit // 2

    def multiply(u, h):
        source = ring(c, offset(u), n_col)
        source_panel = panel if u < n_col - 1 else panel2

        def one_row(w, carry):
            n = source * rd + w
            if u == 0:
                left = panel[pl.ds(r * shard + w * entries, entries)]
            elif u < n_col - 1:
                left = lhs[u - 1, pl.ds(w * entries, entries)]
            else:
                left = lhs[2 + odd, pl.ds(w * entries, entries)]
            left = left.reshape(entries * quarter, left.shape[2])
            right = jnp.concatenate(
                [
                    jnp.concatenate(
                        [source_panel[pick[x, m * group + n]] for x in range(entries)], axis=0
                    )
                    for m in range(cap)
                ],
                axis=1,
            )
            product = lax.dot_general(
                left, right, (((0,), (0,)), ((), ())), preferred_element_type=F32
            ).astype(BF16)
            width = left.shape[1]
            for q in range(n_depth):
                for m in range(cap):
                    part[u, q, w * cap + m] = product[
                        q * quarter : (q + 1) * quarter, m * width : (m + 1) * width
                    ]
            return carry

        lax.fori_loop(h * rows_h, (h + 1) * rows_h, one_row, 0, unroll=True)

    mid = blocks_h // 2

    def mids(h, way):
        return pl.ds(h * blocks_h + way * mid, mid)

    def half_copy(u, h, way):
        return remote(
            part.at[u, ring(d, 2, n_depth), mids(h, way)], half_in.at[u, mids(h, way)],
            h_send.at[u, h, way], h_recv.at[u, h, way], at_depth(signs[way]),
        )

    def full_copy(u, h, way):
        span = pl.ds(h * blocks_h, blocks_h)
        return remote(
            part.at[u, ring(d, signs[way], n_depth), span], full_in.at[u, way, span],
            f_send.at[u, h, way], f_recv.at[u, h, way], at_depth(signs[way]),
        )

    def shift(u):
        return 4 * odd - 2 if u == n_col - 1 else offset(u)

    def back_copy(u, h, kind_of):
        span = pl.ds(kind_of * unit + h * blocks_h, blocks_h)
        return remote(
            part.at[u, d, pl.ds(h * blocks_h, blocks_h)], back.at[span],
            b_send.at[u, h], b_recv.at[u, h], at_col(shift(u)),
        )

    def back_out(u, h):
        return back_copy(u, h, partner if u == n_col - 1 else c)

    def first(u, h):
        for way in range(2):
            half_copy(u, h, way).start()

    def second(u, h):
        for way in range(2):
            half_copy(u, h, way).wait_recv()
            q = ring(d, signs[way], n_depth)
            total = part[u, q, mids(h, way)].astype(F32) + half_in[u, mids(h, way)].astype(F32)
            part[u, q, mids(h, way)] = total.astype(BF16)
            full_copy(u, h, way).start()

    def third(u, h):
        for way in range(2):
            full_copy(u, h, way).wait_recv()
        span = pl.ds(h * blocks_h, blocks_h)
        total = (
            part[u, d, span].astype(F32)
            + full_in[u, 0, span].astype(F32)
            + full_in[u, 1, span].astype(F32)
        ).astype(BF16)
        if u == 0:
            back[pl.ds(c * unit + h * blocks_h, blocks_h)] = total
        else:
            part[u, d, span] = total

    mate_copy = pltpu.make_async_copy(
        lhs.at[mate], panel2.at[pl.ds(r * shard, shard)], local_sem.at[5]
    )
    here = []

    def z_event(t, p):
        z_step(t, p)
        if t == 2:
            here.append(p)
            if len(here) == PIECES:
                mate_copy.start()

    def whole_panel():
        own_copy.wait()
        pick_copy.wait()
        home_copy.wait()
        for h in range(2):
            y4_copy(h, ring(r, 4, n_row)).wait_recv()

    def whole_panel2():
        mate_copy.wait()
        for p in range(PIECES):
            v4_copy(p, ring(r, 4, n_row)).wait_recv()

    def mul(u, h):
        multiply(u, h)
        first(u, h)

    steps = {
        "y": y_step, "z": z_event, "zf": z_first, "v": v_step, "vf": v_first,
        "index": lambda k: index_steps[k](), "panel": whole_panel, "panel2": whole_panel2,
        "mul": mul, "add": second, "end": third,
        "give": lambda u, h: back_out(u, h).start(),
    }
    for step in ORDER:
        steps[step[0]](*step[1:])

    for way in range(2):
        for t in range(1, REACH + 1):
            for h in range(2):
                y_out(way, t, h).wait_send()
            for p in range(PIECES):
                z_copy(way, t, p).wait_send()
                v_out(way, t, p).wait_send()
        for u in range(n_col):
            for h in range(2):
                half_copy(u, h, way).wait_send()
                full_copy(u, h, way).wait_send()
    for h in range(2):
        y4_out(h).wait_send()
        for u in range(1, n_col):
            back_out(u, h).wait_send()
    for p in range(PIECES):
        v4_out(p).wait_send()

    for u in range(1, n_col):
        for h in range(2):
            kind_of = ring(c, -offset(u), n_col)
            back_copy(u, h, kind_of).wait_recv()
    for w in range(rd):
        for a in range(entries):
            out_ref[w * entries + a] = back[home[w, a]]


def solution(mesh):
    n_row, n_col, n_depth = mesh.shape["row"], mesh.shape["col"], mesh.shape["depth"]

    def body(blocks, pattern, place):
        rd, entries, quarter, width = blocks.shape
        nb = pattern.shape[0]
        cap = (entries + n_col - 1) // n_col
        shard, unit = rd * entries, rd * cap
        lanes = cap * rd * n_col
        dma, vmem, ints = pltpu.SemaphoreType.DMA, pltpu.VMEM, jnp.int32
        result = pl.pallas_call(
            functools.partial(kernel, n_row, n_col, n_depth, rd, entries, cap),
            out_shape=jax.ShapeDtypeStruct((shard, quarter, width), BF16),
            in_specs=[pl.BlockSpec(memory_space=pltpu.HBM)] * 3,
            out_specs=pl.BlockSpec(memory_space=pltpu.VMEM),
            scratch_shapes=[
                vmem((n_row * shard + 1, quarter, width), BF16),
                vmem((n_row * shard + 1, quarter, width), BF16),
                vmem((2 * REACH, shard, quarter, width), BF16),
                vmem((n_col, n_depth, unit, quarter, width), BF16),
                vmem((n_col, unit, quarter, width), BF16),
                vmem((n_col, 2, unit, quarter, width), BF16),
                vmem((n_col * unit, quarter, width), BF16),
                vmem((entries, nb), ints), vmem((1, nb), ints), vmem((nb, 16), ints),
                vmem((16, lanes), ints), vmem((8, 128), ints),
                pltpu.SMEM((16, lanes), ints), pltpu.SMEM((8, 128), ints),
                dma((2, 3, 2)), dma((2, 3, 2)), dma((2,)), dma((2,)),
                dma((2, REACH, PIECES)), dma((2, REACH, PIECES)),
                dma((2, 3, PIECES)), dma((2, 3, PIECES)), dma((PIECES,)), dma((PIECES,)),
                dma((n_col, 2, 2)), dma((n_col, 2, 2)),
                dma((n_col, 2, 2)), dma((n_col, 2, 2)),
                dma((n_col, 2)), dma((n_col, 2)),
                dma((6,)),
            ],
            compiler_params=pltpu.CompilerParams(
                collective_id=0, has_side_effects=True, vmem_limit_bytes=48 * 2**20
            ),
        )(*(
            pltpu.with_memory_space_constraint(x, pltpu.HBM)
            for x in (blocks.reshape(shard, quarter, width), pattern.T, place.reshape(1, nb))
        ))
        return result.reshape(blocks.shape)

    placed = (P(("row", "col"), None, "depth", None), P(), P())
    return jax.shard_map(
        body,
        mesh=mesh,
        in_specs=placed,
        out_specs=P(("row", "col"), None, "depth", None),
        check_vma=False,
    )
```

```python
import functools

import jax
import jax.numpy as jnp
from jax import lax
from jax.experimental import pallas as pl
from jax.experimental.pallas import tpu as pltpu
from jax.sharding import PartitionSpec as P

MESH = pl.DeviceIdType.MESH
F32 = jnp.float32
BF16 = jnp.bfloat16
REACH = 3
PIECES = 4

ORDER = (
    ("index", 0), ("index", 1), ("index", 2), ("index", 3), ("y", 1, 0), ("z", 1, 0),
    ("y", 1, 1), ("z", 1, 1), ("y", 2, 0), ("z", 1, 2), ("y", 2, 1), ("z", 1, 3), ("y", 3, 0),
    ("z", 2, 0), ("vf", 0), ("y", 3, 1), ("z", 2, 1), ("vf", 1), ("panel",), ("mul", 1, 0),
    ("v", 1, 0), ("mul", 2, 0), ("mul", 3, 0), ("mul", 4, 0), ("mul", 1, 1), ("mul", 2, 1),
    ("z", 2, 2), ("v", 1, 1), ("add", 1, 0), ("add", 2, 0), ("mul", 0, 0), ("add", 3, 0),
    ("v", 2, 0), ("add", 4, 0), ("add", 1, 1), ("add", 2, 1), ("z", 2, 3), ("v", 2, 1),
    ("end", 1, 0), ("give", 1, 0), ("mul", 3, 1), ("mul", 4, 1), ("end", 2, 0), ("give", 2, 0),
    ("add", 0, 0), ("v", 3, 0), ("vf", 2), ("vf", 3), ("mul", 0, 1), ("z", 3, 0),
    ("end", 3, 0), ("give", 3, 0), ("v", 3, 1), ("end", 4, 0), ("give", 4, 0), ("end", 1, 1),
    ("give", 1, 1), ("end", 2, 1), ("v", 1, 2), ("z", 3, 1), ("add", 3, 1), ("add", 4, 1),
    ("give", 2, 1), ("mul", 5, 0), ("v", 1, 3), ("end", 0, 0), ("mul", 6, 0), ("add", 0, 1),
    ("end", 3, 1), ("z", 3, 2), ("v", 2, 2), ("give", 3, 1), ("end", 4, 1), ("give", 4, 1),
    ("add", 5, 0), ("v", 2, 3), ("add", 6, 0), ("end", 0, 1), ("z", 3, 3), ("mul", 5, 1),
    ("v", 3, 2), ("mul", 6, 1), ("end", 5, 0), ("give", 5, 0), ("end", 6, 0), ("v", 3, 3),
    ("give", 6, 0), ("add", 5, 1), ("add", 6, 1), ("panel2",), ("mul", 7, 0), ("mul", 7, 1),
    ("end", 5, 1), ("give", 5, 1), ("end", 6, 1), ("give", 6, 1), ("add", 7, 0), ("add", 7, 1),
    ("end", 7, 0), ("give", 7, 0), ("end", 7, 1), ("give", 7, 1),
)


def kernel(
    n_row, n_col, n_depth, rd, entries, cap,
    own_ref, pattern_ref, place_ref, out_ref,
    panel, panel2, lhs, part, half_in, full_in, back0, back1,
    pattern_v, place_v, meta, pick_v, home_v, pick, home,
    y_send, y_recv, y4_send, y4_recv, z_send, z_recv,
    v_send, v_recv, v4_send, v4_recv,
    h_send, h_recv, f_send, f_recv, b_send, b_recv, local_sem,
):
    r, c, d = lax.axis_index("row"), lax.axis_index("col"), lax.axis_index("depth")
    core, odd = lax.rem(r, 2), lax.rem(c + 2, 4) // 2
    shard = rd * entries
    piece = shard // PIECES
    half = shard // 2
    group = rd * n_col
    lanes = cap * group
    zero_block = n_row * shard
    unit = rd * cap
    far = n_col // 2

    def ring(me, step, size):
        return lax.rem(me + step + size, size)

    def at_row(step):
        return (ring(r, step, n_row), c, d)

    def at_col(step):
        return (r, ring(c, step, n_col), d)

    def at_depth(step):
        return (r, c, ring(d, step, n_depth))

    def remote(src, dst, send, recv, to):
        return pltpu.make_async_remote_copy(
            src_ref=src, dst_ref=dst, send_sem=send, recv_sem=recv,
            device_id=to, device_id_type=MESH,
        )

    partners = [at_row(1), at_row(-1), at_depth(1), at_depth(-1)]
    partners += [at_col(1), at_col(-1)]
    pattern_copy = pltpu.make_async_copy(pattern_ref, pattern_v, local_sem.at[3])
    place_copy = pltpu.make_async_copy(place_ref, place_v, local_sem.at[4])
    own_copy = pltpu.make_async_copy(
        own_ref, panel.at[pl.ds(r * shard, shard)], local_sem.at[0]
    )
    barrier = pltpu.get_barrier_semaphore()
    for other in partners:
        pl.semaphore_signal(barrier, inc=1, device_id=other, device_id_type=MESH)
    pl.semaphore_wait(barrier, len(partners))

    signs = (1, -1)
    side = 1 - 2 * core

    def span_of(owner, p, size):
        return pl.ds(owner * shard + p * size, size)

    def y_copy(way, t, h, owner_step):
        span = span_of(ring(r, owner_step, n_row), h, half)
        src = own_ref.at[pl.ds(h * half, half)] if t == 1 else panel.at[span]
        return remote(
            src, panel.at[span], y_send.at[way, t - 1, h], y_recv.at[way, t - 1, h],
            at_row(signs[way]),
        )

    def y_out(way, t, h):
        return y_copy(way, t, h, -signs[way] * (t - 1))

    def y_in(way, t, h):
        span = span_of(ring(r, -signs[way] * t, n_row), h, half)
        remote(
            panel.at[span], panel.at[span], y_send.at[way, t - 1, h],
            y_recv.at[way, t - 1, h], at_row(signs[way]),
        ).wait_recv()

    def y4_copy(h, owner):
        span = span_of(owner, h, half)
        return remote(
            panel.at[span], panel.at[span], y4_send.at[h], y4_recv.at[h], at_row(side)
        )

    def y4_out(h):
        return y4_copy(h, ring(r, -3 * side, n_row))

    def y_step(t, h):
        for way in range(2):
            y_in(way, t, h)
            if t < 3:
                y_out(way, t + 1, h).start()
        if t == 3:
            y4_out(h).start()

    mate = 3 - odd

    def v_out(way, t, p):
        span = span_of(ring(r, -signs[way] * (t - 1), n_row), p, piece)
        src = lhs.at[mate, pl.ds(p * piece, piece)] if t == 1 else panel2.at[span]
        return remote(
            src, panel2.at[span], v_send.at[way, t - 1, p], v_recv.at[way, t - 1, p],
            at_row(signs[way]),
        )

    def v_in(way, t, p):
        span = span_of(ring(r, -signs[way] * t, n_row), p, piece)
        remote(
            panel2.at[span], panel2.at[span], v_send.at[way, t - 1, p],
            v_recv.at[way, t - 1, p], at_row(signs[way]),
        ).wait_recv()

    def v4_copy(p, owner):
        span = span_of(owner, p, piece)
        return remote(
            panel2.at[span], panel2.at[span], v4_send.at[p], v4_recv.at[p], at_row(side)
        )

    def v4_out(p):
        return v4_copy(p, ring(r, -3 * side, n_row))

    def v_first(p):
        for way in range(2):
            v_out(way, 1, p).start()

    def v_step(t, p):
        for way in range(2):
            v_in(way, t, p)
            if t < 3:
                v_out(way, t + 1, p).start()
        if t == 3:
            v4_out(p).start()

    def z_copy(way, t, p):
        span = pl.ds(p * piece, piece)
        src = own_ref.at[span] if t == 1 else lhs.at[2 * t - 4 + way, span]
        return remote(
            src, lhs.at[2 * t - 2 + way, span],
            z_send.at[way, t - 1, p], z_recv.at[way, t - 1, p], at_col(signs[way]),
        )

    def z_first(p):
        for way in range(2):
            z_copy(way, 1, p).start()

    def z_step(t, p):
        for way in range(2):
            z_copy(way, t, p).wait_recv()
            if t < REACH:
                z_copy(way, t + 1, p).start()

    for h in range(2):
        z_first(h)
        for way in range(2):
            y_out(way, 1, h).start()
    z_first(2)
    z_first(3)
    pattern_copy.start()
    place_copy.start()
    own_copy.start()
    panel[zero_block] = jnp.zeros((panel.shape[1], panel.shape[2]), BF16)
    panel2[zero_block] = jnp.zeros((panel.shape[1], panel.shape[2]), BF16)

    nb = meta.shape[0]
    partner = ring(c, 2 - 4 * odd, n_col)
    opposite = ring(c, far, n_col)
    visitor = ring(partner, far, n_col)
    pick_copy = pltpu.make_async_copy(pick_v, pick, local_sem.at[1])
    home_copy = pltpu.make_async_copy(home_v, home, local_sem.at[2])
    table = {}

    def index_targets():
        pattern_copy.wait()
        place_copy.wait()
        pad = jnp.zeros((128 - entries - 1, nb), jnp.int32)
        meta[...] = jnp.transpose(
            jnp.concatenate([pattern_v[...], place_v[...], pad], axis=0)
        )[:, : meta.shape[1]]
        lane_of = lax.broadcasted_iota(jnp.int32, (group, lanes), 1) % group
        lane_row = jnp.where(
            lane_of // rd == opposite, lane_of + (visitor - opposite) * rd, lane_of
        )
        pick_row = lax.broadcasted_iota(jnp.int32, (group, lanes), 0) == lane_row
        mine = meta[pl.ds(pl.multiple_of(r * group, group), group), :]
        cols = [
            jnp.sum(jnp.where(pick_row, mine[:, x : x + 1], 0), axis=0, keepdims=True)
            for x in range(entries)
        ]
        lane = lax.broadcasted_iota(jnp.int32, (1, lanes), 1)
        rank = lane // group
        wanted = jnp.where((lane % group) // rd == opposite, partner, c)
        target = jnp.full((1, lanes), -1, jnp.int32)
        seen = jnp.zeros((1, lanes), jnp.int32)
        for x in range(entries):
            hit = lax.rem(cols[x], n_col) == wanted
            target = jnp.where(hit & (seen == rank), cols[x], target)
            seen = seen + hit.astype(jnp.int32)
        ids = lax.broadcasted_iota(jnp.int32, (nb, lanes), 0)
        table["slot"] = jnp.sum(
            jnp.where(ids == target, meta[:, entries : entries + 1], 0), axis=0, keepdims=True
        )
        table["cols"], table["target"] = cols, target
        table["found"] = [jnp.full((1, lanes), zero_block, jnp.int32) for _ in cols]

    def index_matches(low, high):
        slot, cols, target = table["slot"], table["cols"], table["target"]
        at_slot = lax.broadcasted_iota(jnp.int32, (nb, lanes), 0) == slot
        base = (slot // group * rd + lax.rem(slot, rd)) * entries
        for y in range(low, high):
            far_col = jnp.sum(
                jnp.where(at_slot, meta[:, y : y + 1], 0), axis=0, keepdims=True
            )
            table["found"] = [
                jnp.where((cols[x] == far_col) & (target >= 0), base + y, table["found"][x])
                for x in range(entries)
            ]

    def index_home():
        for x in range(entries):
            pick_v[pl.ds(x, 1), :] = table["found"][x]
        own_rows = meta[pl.ds(pl.multiple_of((r * n_col + c) * rd, rd), rd), :]
        width = own_rows.shape[1]
        kind = lax.rem(own_rows, n_col)
        entry = lax.broadcasted_iota(jnp.int32, (rd, width), 1)
        before = jnp.zeros((rd, width), jnp.int32)
        for x in range(entries):
            before = before + ((kind == kind[:, x : x + 1]) & (entry > x)).astype(jnp.int32)
        row = lax.broadcasted_iota(jnp.int32, (rd, width), 0)
        home_v[:, pl.ds(0, width)] = kind * (unit // 2) + lax.rem(row, rd // 2) * cap + before
        pick_copy.start()
        home_copy.start()

    index_steps = (
        index_targets,
        lambda: index_matches(0, entries // 2),
        lambda: index_matches(entries // 2, entries),
        index_home,
    )

    def offset(u):
        t = (u + 1) // 2
        return 0 if u == 0 else (far if t == far else (-t if u % 2 == 1 else t))

    backs = (back0, back1)
    quarter = panel.shape[1]
    rows_h = rd // 2
    blocks_h = unit // 2

    def multiply(u, h):
        source = ring(c, offset(u), n_col)
        source_panel = panel if u < n_col - 1 else panel2

        def one_row(w, carry):
            n = source * rd + w
            if u == 0:
                left = panel[pl.ds(r * shard + w * entries, entries)]
            elif u < n_col - 1:
                left = lhs[u - 1, pl.ds(w * entries, entries)]
            else:
                left = lhs[2 + odd, pl.ds(w * entries, entries)]
            left = left.reshape(entries * quarter, left.shape[2])
            right = jnp.concatenate(
                [
                    jnp.concatenate(
                        [source_panel[pick[x, m * group + n]] for x in range(entries)], axis=0
                    )
                    for m in range(cap)
                ],
                axis=1,
            )
            product = lax.dot_general(
                left, right, (((0,), (0,)), ((), ())), preferred_element_type=F32
            ).astype(BF16)
            width = left.shape[1]
            for q in range(n_depth):
                for m in range(cap):
                    part[u, q, w * cap + m] = product[
                        q * quarter : (q + 1) * quarter, m * width : (m + 1) * width
                    ]
            return carry

        lax.fori_loop(h * rows_h, (h + 1) * rows_h, one_row, 0, unroll=True)

    mid = blocks_h // 2

    def mids(h, way):
        return pl.ds(h * blocks_h + way * mid, mid)

    def half_copy(u, h, way):
        return remote(
            part.at[u, ring(d, 2, n_depth), mids(h, way)], half_in.at[u, mids(h, way)],
            h_send.at[u, h, way], h_recv.at[u, h, way], at_depth(signs[way]),
        )

    def full_copy(u, h, way):
        span = pl.ds(h * blocks_h, blocks_h)
        return remote(
            part.at[u, ring(d, signs[way], n_depth), span], full_in.at[u, way, span],
            f_send.at[u, h, way], f_recv.at[u, h, way], at_depth(signs[way]),
        )

    def shift(u):
        return 4 * odd - 2 if u == n_col - 1 else offset(u)

    def back_copy(u, h, kind_of):
        span = pl.ds(kind_of * blocks_h, blocks_h)
        return remote(
            part.at[u, d, pl.ds(h * blocks_h, blocks_h)], backs[h].at[span],
            b_send.at[u, h], b_recv.at[u, h], at_col(shift(u)),
        )

    def back_out(u, h):
        return back_copy(u, h, partner if u == n_col - 1 else c)

    def first(u, h):
        for way in range(2):
            half_copy(u, h, way).start()

    def second(u, h):
        for way in range(2):
            half_copy(u, h, way).wait_recv()
            q = ring(d, signs[way], n_depth)
            total = part[u, q, mids(h, way)].astype(F32) + half_in[u, mids(h, way)].astype(F32)
            part[u, q, mids(h, way)] = total.astype(BF16)
            full_copy(u, h, way).start()

    def third(u, h):
        for way in range(2):
            full_copy(u, h, way).wait_recv()
        span = pl.ds(h * blocks_h, blocks_h)
        total = (
            part[u, d, span].astype(F32)
            + full_in[u, 0, span].astype(F32)
            + full_in[u, 1, span].astype(F32)
        ).astype(BF16)
        if u == 0:
            backs[h][pl.ds(c * blocks_h, blocks_h)] = total
        else:
            part[u, d, span] = total

    mate_copy = pltpu.make_async_copy(
        lhs.at[mate], panel2.at[pl.ds(r * shard, shard)], local_sem.at[5]
    )
    here = []

    def z_event(t, p):
        z_step(t, p)
        if t == 2:
            here.append(p)
            if len(here) == PIECES:
                mate_copy.start()

    def whole_panel():
        own_copy.wait()
        pick_copy.wait()
        home_copy.wait()
        for h in range(2):
            y4_copy(h, ring(r, 4, n_row)).wait_recv()

    def whole_panel2():
        mate_copy.wait()
        for p in range(PIECES):
            v4_copy(p, ring(r, 4, n_row)).wait_recv()

    def mul(u, h):
        multiply(u, h)
        first(u, h)

    steps = {
        "y": y_step, "z": z_event, "zf": z_first, "v": v_step, "vf": v_first,
        "index": lambda k: index_steps[k](), "panel": whole_panel, "panel2": whole_panel2,
        "mul": mul, "add": second, "end": third,
        "give": lambda u, h: back_out(u, h).start(),
    }
    for step in ORDER:
        steps[step[0]](*step[1:])

    for way in range(2):
        for t in range(1, REACH + 1):
            for h in range(2):
                y_out(way, t, h).wait_send()
            for p in range(PIECES):
                z_copy(way, t, p).wait_send()
                v_out(way, t, p).wait_send()
        for u in range(n_col):
            for h in range(2):
                half_copy(u, h, way).wait_send()
                full_copy(u, h, way).wait_send()
    for h in range(2):
        y4_out(h).wait_send()
        for u in range(1, n_col):
            back_out(u, h).wait_send()
    for p in range(PIECES):
        v4_out(p).wait_send()

    for h in range(2):
        for u in range(1, n_col):
            back_copy(u, h, ring(c, -offset(u), n_col)).wait_recv()
        for w in range(h * rows_h, (h + 1) * rows_h):
            for a in range(entries):
                out_ref[w * entries + a] = backs[h][home[w, a]]


def solution(mesh):
    n_row, n_col, n_depth = mesh.shape["row"], mesh.shape["col"], mesh.shape["depth"]

    def body(blocks, pattern, place):
        rd, entries, quarter, width = blocks.shape
        nb = pattern.shape[0]
        cap = (entries + n_col - 1) // n_col
        shard, unit = rd * entries, rd * cap
        lanes = cap * rd * n_col
        dma, vmem, ints = pltpu.SemaphoreType.DMA, pltpu.VMEM, jnp.int32
        result = pl.pallas_call(
            functools.partial(kernel, n_row, n_col, n_depth, rd, entries, cap),
            out_shape=jax.ShapeDtypeStruct((shard, quarter, width), BF16),
            in_specs=[pl.BlockSpec(memory_space=pltpu.HBM)] * 3,
            out_specs=pl.BlockSpec(memory_space=pltpu.VMEM),
            scratch_shapes=[
                vmem((n_row * shard + 1, quarter, width), BF16),
                vmem((n_row * shard + 1, quarter, width), BF16),
                vmem((2 * REACH, shard, quarter, width), BF16),
                vmem((n_col, n_depth, unit, quarter, width), BF16),
                vmem((n_col, unit, quarter, width), BF16),
                vmem((n_col, 2, unit, quarter, width), BF16),
                vmem((n_col * unit // 2, quarter, width), BF16),
                vmem((n_col * unit // 2, quarter, width), BF16),
                vmem((entries, nb), ints), vmem((1, nb), ints), vmem((nb, 16), ints),
                vmem((16, lanes), ints), vmem((8, 128), ints),
                pltpu.SMEM((16, lanes), ints), pltpu.SMEM((8, 128), ints),
                dma((2, 3, 2)), dma((2, 3, 2)), dma((2,)), dma((2,)),
                dma((2, REACH, PIECES)), dma((2, REACH, PIECES)),
                dma((2, 3, PIECES)), dma((2, 3, PIECES)), dma((PIECES,)), dma((PIECES,)),
                dma((n_col, 2, 2)), dma((n_col, 2, 2)),
                dma((n_col, 2, 2)), dma((n_col, 2, 2)),
                dma((n_col, 2)), dma((n_col, 2)),
                dma((6,)),
            ],
            compiler_params=pltpu.CompilerParams(
                collective_id=0, has_side_effects=True, vmem_limit_bytes=48 * 2**20
            ),
        )(*(
            pltpu.with_memory_space_constraint(x, pltpu.HBM)
            for x in (blocks.reshape(shard, quarter, width), pattern.T, place.reshape(1, nb))
        ))
        return result.reshape(blocks.shape)

    placed = (P(("row", "col"), None, "depth", None), P(), P())
    return jax.shard_map(
        body,
        mesh=mesh,
        in_specs=placed,
        out_specs=P(("row", "col"), None, "depth", None),
        check_vma=False,
    )
```
